32 devices in a mesh: groups: 2 (over y), blk: 16 (over z, x, core).
Axes of the slice: x: 2, y: 2, z: 4, core: 2. Of those that a mesh axis runs over, the one named last changes fastest.
Arguments:
- tokens: bfloat16 [4096, 16384], P(('groups', 'blk')), parts along dimension 0, may hold values from -6 to 6
- gain: float32 [16384], replicated, may hold values from 0.1 to 1.9
- w_query: bfloat16 [16384, 256], P('blk'), may hold values from -0.046875 to 0.046875
- w_key_value: bfloat16 [16384, 256], P('blk'), may hold values from -0.046875 to 0.046875
- w_out: bfloat16 [256, 16384], P(None, 'blk'), may hold values from -0.375 to 0.375
- cache_kv: bfloat16 [32, 8192, 256], P(('groups', 'blk')), parts along dimension 0, may hold values from -288 to 288
- cached_len: int32 [32], P('groups'), parts along dimension 0, may hold values from 1 to 8192, as said below
Outputs:
- mixed: bfloat16 [4096, 16384], P(('groups', 'blk')), parts along dimension 0
The draws below stay inside these ranges and needn't reach their ends.
There are 2 independent parts, one for each index of `groups`. The reference program is written for one: setup_inputs(seed, part) draws one part's arguments, and reference() takes and returns one part's arrays. A program takes and returns all parts, laid end to end along the dimension named above; an argument that names none is the same for every part. Nothing has to cross between parts.
Inputs may be any that keep to these rules, and one draw needn't show every extreme that they name: `cached_len`: in every draw some prompt has all 8192 slots cached.
All inputs are finite; a program needn't handle non-finite values.
Results may differ from the reference program's by a relative error of at most 0.0065.
Values may be sent and summed in bfloat16 or wider, within the bound.
No kernel may reach another device: no remote copies, remote signals or barrier semaphores. Data moves between devices by JAX's collectives and lax.ppermute only.
A program may use at most 128 MiB of HBM per device.

```python
import jax
import jax.numpy as jnp
from jax import lax

D = 16384
HEAD = 128
QH = 2
LEN = 128
CACHE = 8192
PROMPTS = 16
TOKENS = 2048


def draw_cache_kv(key, part):
    key = jax.random.fold_in(key, 11)
    first = jax.random.fold_in(key, 0)
    shape = (PROMPTS, CACHE, 2 * HEAD)
    base = jnp.clip(jax.random.normal(first, shape, jnp.float32), -6.0, 6.0)
    return base.astype(jnp.bfloat16)


def draw_cached_len(key, part):
    key = jax.random.fold_in(key, 5)
    first, second = jax.random.split(key)
    lengths = jax.random.randint(first, (PROMPTS,), 1, CACHE + 1)
    chosen = jax.random.randint(second, (), 0, PROMPTS)
    return jnp.where(jnp.arange(PROMPTS) == chosen, CACHE, lengths).astype(jnp.int32)


def block_levels(stream_key, dims, cuts, low, largest):
    def one(position, blocks):
        heights = jax.random.uniform(jax.random.fold_in(jax.random.fold_in(stream_key, 6), position), (blocks,), jnp.float32, low / len(cuts), largest / len(cuts))
        return jnp.repeat(jnp.exp(heights), dims[position] // blocks).reshape((-1,) + (1,) * (len(dims) - position - 1))

    level = one(*cuts[0])
    for cut in cuts[1:]:
        level = level * one(*cut)
    return level


def normal_values(key, extent, spread, bound, cuts=(), held_as=jnp.bfloat16):
    values = spread * jax.random.normal(key, extent, jnp.float32)
    if cuts:
        values = values * block_levels(key, extent, cuts, -0.22, 0.18)
    return jnp.clip(values, -bound, bound).astype(held_as)


def setup_inputs(seed: int = 0, part: int = 0) -> dict:
    arg_keys = jax.random.split(jax.random.key(seed), 8)
    part_keys = jax.random.split(jax.random.fold_in(arg_keys[7], part), 8)
    tokens = normal_values(part_keys[0], (TOKENS, D), 1.0, 6.0, ((0, 16),))
    gain = jnp.clip(1.0 + 0.18 * jax.random.normal(arg_keys[1], (D,), jnp.float32), 0.1, 1.9)
    w_query = normal_values(arg_keys[2], (D, QH * HEAD), D ** -0.5, 0.046875, ((0, 16),))
    w_key_value = normal_values(arg_keys[3], (D, 2 * HEAD), D ** -0.5, 0.046875, ((0, 16),))
    w_out = normal_values(arg_keys[4], (QH * HEAD, D), (QH * HEAD) ** -0.5, 0.375, ((1, 16),))
    cache_kv = draw_cache_kv(jax.random.fold_in(jax.random.fold_in(arg_keys[7], part), 71), part)
    cached_len = draw_cached_len(jax.random.fold_in(jax.random.fold_in(arg_keys[7], part), 71), part)
    return {"tokens": tokens, "gain": gain, "w_query": w_query, "w_key_value": w_key_value, "w_out": w_out, "cache_kv": cache_kv, "cached_len": cached_len}


def rotate(values, positions):
    half_size = values.shape[-1] // 2
    steps = jnp.arange(half_size, dtype=jnp.float32) * (2.0 / values.shape[-1])
    freqs = jnp.exp(-jnp.log(jnp.float32(500000.0)) * steps)
    angles = positions[:, None] * freqs[None, :]
    cosine = jnp.cos(angles)[:, None, :]
    sine = jnp.sin(angles)[:, None, :]
    first = values[..., :half_size]
    second = values[..., half_size:]
    return jnp.concatenate([first * cosine - second * sine, second * cosine + first * sine], axis=-1)

def reference(tokens, gain, w_query, w_key_value, w_out, cache_kv, cached_len):
    prompt_rows = tokens.reshape(PROMPTS, LEN, D)

    def one_prompt(items):
        rows, cache, length = items
        widened = rows.astype(jnp.float32)
        normed = (widened * lax.rsqrt(lax.optimization_barrier(jnp.mean(widened * widened, axis=-1, keepdims=True)) + 1e-05) * gain).astype(jnp.bfloat16)
        query = jnp.dot(normed, w_query, preferred_element_type=jnp.float32)
        keyval = jnp.dot(normed, w_key_value, preferred_element_type=jnp.float32)
        positions = length.astype(jnp.float32) + jnp.arange(LEN, dtype=jnp.float32)
        q_rot = rotate(query.reshape(LEN, QH, HEAD), positions).astype(jnp.bfloat16)
        k_rot = rotate(keyval[:, None, :HEAD], positions)[:, 0, :].astype(jnp.bfloat16)
        val = keyval[:, HEAD:].astype(jnp.bfloat16)
        keys = jnp.concatenate([cache[:, :HEAD], k_rot], axis=0)
        values = jnp.concatenate([cache[:, HEAD:], val], axis=0)
        scores = jnp.einsum('tqh,kh->qtk', q_rot.astype(jnp.float32), keys.astype(jnp.float32)) * HEAD ** (-0.5)
        slots = jnp.arange(CACHE, dtype=jnp.int32)
        cache_mask = jnp.broadcast_to((slots < length)[None, :], (LEN, CACHE))
        steps_new = jnp.arange(LEN, dtype=jnp.int32)
        own_mask = steps_new[None, :] <= steps_new[:, None]
        mask = jnp.concatenate([cache_mask, own_mask], axis=1)[None, :, :]
        scores = jnp.where(mask, scores, -1e+30)
        top = lax.optimization_barrier(jnp.max(scores, axis=-1, keepdims=True))
        expo = jnp.where(mask, jnp.exp(scores - top), 0.0)
        weights = (expo / lax.optimization_barrier(jnp.sum(expo, axis=-1, keepdims=True))).astype(jnp.bfloat16)
        attended = jnp.einsum('qtk,kh->tqh', weights.astype(jnp.float32), values.astype(jnp.float32))
        attended = attended.astype(jnp.bfloat16).reshape(LEN, QH * HEAD)
        projected = jnp.dot(attended, w_out, preferred_element_type=jnp.float32)
        return (widened + projected).astype(jnp.bfloat16)
    mixed = lax.map(one_prompt, (prompt_rows, cache_kv, cached_len))
    return mixed.reshape(TOKENS, D)
```

```python
import functools

import jax
import jax.numpy as jnp
from jax import lax
from jax.experimental import pallas as pl
from jax.experimental.pallas import tpu as pltpu
from jax.sharding import Mesh, PartitionSpec as P

F32 = jnp.float32
BF16 = jnp.bfloat16
AXES = ("y", "z", "r", "x", "c")
VMEM_LIMIT = 56 * 1024 * 1024


def params():
    return pltpu.CompilerParams(vmem_limit_bytes=VMEM_LIMIT)


def norm_kernel(idx, tok, gain, *outs, nz, nr, bs):
    x, c = idx[1], idx[2]
    width = tok.shape[1]
    step = 1024
    for r0 in range(0, tok.shape[0], 16):
        rows = pl.ds(r0, 16)
        acc = jnp.zeros((16, step), F32)
        for j in range(width // step):
            v = tok[rows, pl.ds(j * step, step)].astype(F32)
            acc = acc + v * v
        inv = lax.rsqrt(jnp.sum(acc, axis=1, keepdims=True) * (1.0 / width) + 1e-05)
        for k, out in enumerate(outs):
            part = (x ^ (k // 2)) * 2 + (c ^ (k % 2))
            for g in range(nz * nr):
                cols = pl.ds(pl.multiple_of((g * 4 + part) * bs, bs), bs)
                v = tok[rows, cols].astype(F32) * inv * gain[:, cols]
                out[rows, pl.ds(g * bs, bs)] = v.astype(BF16)


def normalise(idx, tokens, gain, nz, nr, bs):
    rows, width = tokens.shape
    block = 32
    quarter = width // 4
    return pl.pallas_call(
        functools.partial(norm_kernel, nz=nz, nr=nr, bs=bs),
        grid_spec=pltpu.PrefetchScalarGridSpec(
            num_scalar_prefetch=1,
            grid=(rows // block,),
            in_specs=[
                pl.BlockSpec((block, width), lambda i, s: (i, 0)),
                pl.BlockSpec((1, width), lambda i, s: (0, 0)),
            ],
            out_specs=[pl.BlockSpec((block, quarter), lambda i, s: (i, 0))] * 4,
        ),
        out_shape=[jax.ShapeDtypeStruct((rows, quarter), BF16)] * 4,
        compiler_params=params(),
        cost_estimate=pl.CostEstimate(flops=8 * rows * width, bytes_accessed=4 * rows * width, transcendentals=0),
        name="norm",
    )(idx, tokens, gain.reshape(1, width))


def project_kernel(idx, *refs, nz, half, lead):
    toks, refs = refs[:4], refs[4:]
    own_q, own_kv = refs[:2]
    near = refs[2 : 2 + nz - 1]
    far = refs[2 + nz - 1 : 2 * nz]
    outs = refs[2 * nz : 2 * nz + 4]
    tbuf, wbuf, qbuf, tsem, wsem = refs[2 * nz + 4 :]
    y, z = idx[3], idx[0]
    copies = []
    for i in range(4):
        copies.append(pltpu.make_async_copy(toks[i], tbuf.at[i], tsem.at[i]))
    own = [
        pltpu.make_async_copy(own_q, qbuf.at[0], wsem.at[0]),
        pltpu.make_async_copy(own_kv, qbuf.at[1], wsem.at[1]),
    ]
    rest = [
        pltpu.make_async_copy(ref, wbuf.at[i], wsem.at[2 + i]) for i, ref in enumerate(list(near) + list(far))
    ]
    for cp in own + copies + rest:
        cp.start()
    for cp in own + copies:
        cp.wait()
    start = pl.multiple_of(z * 2 * half, 2 * half)
    for i in range(4):
        t = tbuf[i, :, pl.ds(start, 2 * half)]
        outs[i][:, :lead] = jnp.dot(t, qbuf[0], preferred_element_type=F32)
        outs[i][:, lead:] = jnp.dot(t, qbuf[1], preferred_element_type=F32)
    for n in range(2 * (nz - 1)):
        rest[n].wait()
        s = n % (nz - 1) + 1
        side = y if n < nz - 1 else 1 - y
        start = pl.multiple_of(lax.rem(z - s + nz, nz) * 2 * half + side * half, half)
        w = wbuf[n]
        for i in range(4):
            outs[i][...] += jnp.dot(tbuf[i, :, pl.ds(start, half)], w, preferred_element_type=F32)


def project(idx, toks, own_q, own_kv, near, far):
    nz = len(near) + 1
    rows = toks[0].shape[0]
    half, width = near[0].shape
    anywhere = pl.BlockSpec(memory_space=pl.ANY)
    lead = own_q.shape[1]
    return pl.pallas_call(
        functools.partial(project_kernel, nz=nz, half=half, lead=lead),
        in_specs=[pl.BlockSpec(memory_space=pltpu.SMEM)] + [anywhere] * (4 + 2 * nz),
        out_specs=[pl.BlockSpec(memory_space=pltpu.VMEM)] * 4,
        out_shape=[jax.ShapeDtypeStruct((rows, width), F32)] * 4,
        scratch_shapes=[
            pltpu.VMEM((4,) + toks[0].shape, BF16),
            pltpu.VMEM((2 * (nz - 1), half, width), BF16),
            pltpu.VMEM((2, 2 * half, lead), BF16),
            pltpu.SemaphoreType.DMA((4,)),
            pltpu.SemaphoreType.DMA((2 * nz,)),
        ],
        compiler_params=params(),
        cost_estimate=pl.CostEstimate(
            flops=2 * 4 * rows * toks[0].shape[1] * width, bytes_accessed=16 * 1024 * 1024, transcendentals=0
        ),
        name="project",
    )(idx, *toks, own_q, own_kv, *near, *far)


def attend_kernel(idx, mine, other, cos, sin, cache, out, kvbuf, sem, *, heads, head):
    length = idx[4]
    slots = kvbuf.shape[0]
    rows = mine.shape[0]
    chunk = 1024
    copies = [
        pltpu.make_async_copy(
            cache.at[0, pl.ds(i * chunk, chunk)], kvbuf.at[pl.ds(i * chunk, chunk)], sem.at[i]
        )
        for i in range(slots // chunk)
    ]
    for cp in copies:
        cp.start()
    total = mine[...] + other[...]

    def turn(v):
        return (v * cos[...] + pltpu.roll(v, head // 2, 1) * sin[...]).astype(BF16)

    q = jnp.concatenate([turn(total[:, i * head : (i + 1) * head]) for i in range(heads)], axis=0)
    k_new = turn(total[:, heads * head : (heads + 1) * head])
    v_new = total[:, (heads + 1) * head :].astype(BF16)
    scale = (head ** -0.5) * 1.4426950408889634

    def scores(keys):
        return lax.dot_general(q, keys, (((1,), (1,)), ((), ())), preferred_element_type=F32)

    s = scores(k_new)
    row = lax.broadcasted_iota(jnp.int32, s.shape, 0) % rows
    col = lax.broadcasted_iota(jnp.int32, s.shape, 1)
    s = jnp.where(col <= row, s, -1e30)
    top = jnp.max(s, axis=1, keepdims=True)
    p = jnp.exp2((s - top) * scale)
    total_p = jnp.sum(p, axis=1, keepdims=True)
    acc = jnp.dot(p.astype(BF16), v_new, preferred_element_type=F32)
    for i, cp in enumerate(copies):
        cp.wait()
        s = scores(kvbuf[pl.ds(i * chunk, chunk), :head])
        col = lax.broadcasted_iota(jnp.int32, (1, chunk), 1) + i * chunk
        s = jnp.where(col < length, s, -1e30)
        new_top = jnp.maximum(top, jnp.max(s, axis=1, keepdims=True))
        p = jnp.exp2((s - new_top) * scale)
        fade = jnp.exp2((top - new_top) * scale)
        top = new_top
        total_p = total_p * fade + jnp.sum(p, axis=1, keepdims=True)
        acc = acc * fade + jnp.dot(
            p.astype(BF16), kvbuf[pl.ds(i * chunk, chunk), head:], preferred_element_type=F32
        )
    acc = (acc / total_p).astype(BF16)
    for i in range(heads):
        out[:, i * head : (i + 1) * head] = acc[i * rows : (i + 1) * rows]


def attend(idx, mine, other, cos, sin, cache, heads, head):
    vmem = pl.BlockSpec(memory_space=pltpu.VMEM)
    rows = mine.shape[0]
    slots = cache.shape[1]
    return pl.pallas_call(
        functools.partial(attend_kernel, heads=heads, head=head),
        in_specs=[pl.BlockSpec(memory_space=pltpu.SMEM)] + [vmem] * 4 + [pl.BlockSpec(memory_space=pl.ANY)],
        out_specs=vmem,
        out_shape=jax.ShapeDtypeStruct((rows, heads * head), BF16),
        scratch_shapes=[pltpu.VMEM(cache.shape[1:], BF16), pltpu.SemaphoreType.DMA((slots // 1024,))],
        compiler_params=params(),
        cost_estimate=pl.CostEstimate(
            flops=4 * rows * heads * head * slots, bytes_accessed=12 * 1024 * 1024, transcendentals=rows * heads * slots
        ),
        name="attend",
    )(idx, mine, other, cos, sin, cache)


def out_kernel(idx, att, tok, *refs, plan, nz, nr, bs):
    n = len(refs) - 6 - 1
    weights, out = refs[:n], refs[n]
    wbuf, tbuf, obuf, wsem, tsem, osem = refs[n + 1 :]
    z, x, c, y = idx[0], idx[1], idx[2], idx[3]
    half = att.shape[1] // 2
    rows = att.shape[0]
    flip = y == 1
    low, high = att[:, :half], att[:, half:]
    left = jnp.concatenate([jnp.where(flip, high, low), jnp.where(flip, low, high)], axis=1)
    slots = wbuf.shape[0]

    def cols(s, dx, dc, r):
        zz = lax.rem(z - s + nz, nz)
        return pl.ds(pl.multiple_of(((zz * nr + r) * 4 + (x ^ dx) * 2 + (c ^ dc)) * bs, bs), bs)

    def load(b):
        (s, dx, dc), halves = plan[b]
        slot = b % slots
        cps = []
        for h, (ref, lead, pos) in enumerate(halves):
            src = weights[ref] if lead is None else weights[ref].at[lead]
            if pos is not None:
                side = y if pos == 0 else 1 - y
                src = src.at[pl.ds(pl.multiple_of(side * half, half), half)]
            cps.append(pltpu.make_async_copy(src, wbuf.at[slot, pl.ds(h * half, half)], wsem.at[slot, h]))
        for r in range(nr):
            cps.append(
                pltpu.make_async_copy(tok.at[:, cols(s, dx, dc, r)], tbuf.at[slot, :, pl.ds(r * bs, bs)], tsem.at[slot, r])
            )
        return cps

    def store(b):
        (s, dx, dc), _ = plan[b]
        slot = b % slots
        return [
            pltpu.make_async_copy(obuf.at[slot, :, pl.ds(r * bs, bs)], out.at[:, cols(s, dx, dc, r)], osem.at[slot, r])
            for r in range(nr)
        ]

    for b in range(min(slots, len(plan))):
        for cp in load(b):
            cp.start()
    for b in range(len(plan)):
        slot = b % slots
        for cp in load(b):
            cp.wait()
        if b >= slots:
            for cp in store(b - slots):
                cp.wait()
        v = jnp.dot(left, wbuf[slot], preferred_element_type=F32)
        obuf[slot] = (tbuf[slot].astype(F32) + v).astype(BF16)
        for cp in store(b):
            cp.start()
        if b + slots < len(plan):
            for cp in load(b + slots):
                cp.start()
    for b in range(max(0, len(plan) - slots), len(plan)):
        for cp in store(b):
            cp.wait()


def output(idx, att, tokens, weights, plan, nz, nr, bs):
    anywhere = pl.BlockSpec(memory_space=pl.ANY)
    slots = 4
    rows, width = tokens.shape
    return pl.pallas_call(
        functools.partial(out_kernel, plan=plan, nz=nz, nr=nr, bs=bs),
        in_specs=[pl.BlockSpec(memory_space=pltpu.SMEM), pl.BlockSpec(memory_space=pltpu.VMEM)]
        + [anywhere] * (1 + len(weights)),
        out_specs=anywhere,
        out_shape=jax.ShapeDtypeStruct(tokens.shape, BF16),
        scratch_shapes=[
            pltpu.VMEM((slots, att.shape[1], nr * bs), BF16),
            pltpu.VMEM((slots, rows, nr * bs), BF16),
            pltpu.VMEM((slots, rows, nr * bs), BF16),
            pltpu.SemaphoreType.DMA((slots, 2)),
            pltpu.SemaphoreType.DMA((slots, nr)),
            pltpu.SemaphoreType.DMA((slots, nr)),
        ],
        compiler_params=params(),
        cost_estimate=pl.CostEstimate(
            flops=2 * rows * width * att.shape[1], bytes_accessed=16 * 1024 * 1024, transcendentals=0
        ),
        name="output",
    )(idx, att, tokens, *weights)


def body(tokens, gain, w_query, w_key_value, w_out, cache_kv, cached_len, *, nz, nr):
    rows = tokens.shape[0]
    head = w_key_value.shape[1] // 2
    heads = w_query.shape[1] // head
    bs = w_query.shape[0]
    y, z, x, c = (lax.axis_index(a) for a in ("y", "z", "x", "c"))
    prompt = ((z * nr + lax.axis_index("r")) * 2 + x) * 2 + c
    length = jnp.sum(jnp.where(jnp.arange(cached_len.shape[0], dtype=jnp.int32) == prompt, cached_len, 0))
    idx = jnp.stack([z, x, c, y, length]).astype(jnp.int32)

    def swap(v, axis):
        return lax.ppermute(v, axis, [(0, 1), (1, 0)])

    def across(v):
        return lax.ppermute(v, ("x", "c"), [(i, i ^ 3) for i in range(4)])

    def ring(v):
        return lax.ppermute(v, "z", [(i, (i + 1) % nz) for i in range(nz)])

    own_q, own_kv, own_o = w_query, w_key_value, w_out
    if nr > 1:
        own_q = lax.all_gather(own_q, "r", axis=0, tiled=True)
        own_kv = lax.all_gather(own_kv, "r", axis=0, tiled=True)
        own_o = lax.all_gather(own_o, "r", axis=1, tiled=True)
    half = own_q.shape[0] // 2
    ohalf = own_o.shape[0] // 2

    w_near = [
        jnp.concatenate(
            [lax.dynamic_slice_in_dim(own_q, y * half, half), lax.dynamic_slice_in_dim(own_kv, y * half, half)], axis=1
        )
    ]
    o_mine = lax.dynamic_slice_in_dim(own_o, y * ohalf, ohalf)
    o_else = lax.dynamic_slice_in_dim(own_o, (1 - y) * ohalf, ohalf)
    o_mine_x = swap(o_mine, "x")
    toks = normalise(idx, tokens, gain, nz, nr, bs)
    w_far = []
    o_near = [jnp.stack([o_mine, o_mine_x])]
    o_far = []
    for s in range(1, nz):
        w_near.append(ring(w_near[-1]))
        w_far.append(swap(w_near[-1], "y"))
        o_near.append(ring(o_near[-1]))
        o_far.append(swap(o_near[-1], "y"))
    held = [toks[0], swap(toks[1], "c"), swap(toks[2], "x"), across(toks[3])]
    parts = project(idx, held, own_q, own_kv, w_near[1:], w_far)
    from_c0 = swap(parts[1], "c")
    from_c1 = swap(parts[3], "c")
    other = swap(parts[2] + from_c1, "x")
    o_else_x = swap(o_else, "x")
    mine = parts[0] + from_c0

    positions = length.astype(F32) + jnp.arange(rows, dtype=F32)
    steps = jnp.arange(head // 2, dtype=F32) * (2.0 / head)
    freqs = jnp.exp(-jnp.log(jnp.float32(500000.0)) * steps)
    angles = positions[:, None] * freqs[None, :]
    cos, sin = jnp.cos(angles), jnp.sin(angles)
    att = attend(
        idx,
        mine,
        other,
        jnp.concatenate([cos, cos], axis=1),
        jnp.concatenate([-sin, sin], axis=1),
        cache_kv,
        heads,
        head,
    )

    weights, plan = [], []

    def add(v):
        weights.append(v)
        return len(weights) - 1

    for dc in range(2):
        over = (lambda v: swap(v, "c")) if dc else (lambda v: v)
        own = add(over(own_o))
        mx, ex = add(over(o_mine_x)), add(over(o_else_x))
        plan.append(((0, 0, dc), [(own, None, 0), (own, None, 1)]))
        plan.append(((0, 1, dc), [(mx, None, None), (ex, None, None)]))
    for s in range(1, nz):
        for dc in range(2):
            over = (lambda v: swap(v, "c")) if dc else (lambda v: v)
            near, far = add(over(o_near[s])), add(over(o_far[s - 1]))
            for dx in range(2):
                plan.append(((s, dx, dc), [(near, dx, None), (far, dx, None)]))
    return output(idx, att, tokens, weights, plan, nz, nr, bs)


def solution(mesh):
    groups, blk = mesh.shape["groups"], mesh.shape["blk"]
    nz = 4
    nr = blk // (4 * nz)
    wide = Mesh(mesh.devices.reshape(groups, nz, nr, 2, 2), AXES)
    blocks = ("z", "r", "x", "c")
    placed = (
        P(AXES, None),
        P(),
        P(blocks, None),
        P(blocks, None),
        P(None, blocks),
        P(AXES, None, None),
        P("y"),
    )
    return jax.shard_map(
        functools.partial(body, nz=nz, nr=nr),
        mesh=wide,
        in_specs=placed,
        out_specs=P(AXES, None),
        check_vma=False,
    )
```

```python
import functools

import jax
import jax.numpy as jnp
from jax import lax
from jax.experimental import pallas as pl
from jax.experimental.pallas import tpu as pltpu
from jax.sharding import Mesh, PartitionSpec as P

F32 = jnp.float32
BF16 = jnp.bfloat16
AXES = ("y", "z", "r", "x", "c")
VMEM_LIMIT = 56 * 1024 * 1024


def params():
    return pltpu.CompilerParams(vmem_limit_bytes=VMEM_LIMIT)


def norm_kernel(tok, gain, *outs, nz, nr, bs):
    z, x, c = (lax.axis_index(a) for a in ("z", "x", "c"))
    width = tok.shape[1]
    step = 1024
    for r0 in range(0, tok.shape[0], 16):
        rows = pl.ds(r0, 16)
        acc = jnp.zeros((16, step), F32)
        for j in range(width // step):
            v = tok[rows, pl.ds(j * step, step)].astype(F32)
            acc = acc + v * v
        inv = lax.rsqrt(jnp.sum(acc, axis=1, keepdims=True) * (1.0 / width) + 1e-05)
        for k, out in enumerate(outs):
            part = (x ^ (k // 2)) * 2 + (c ^ (k % 2))
            for s in range(nz):
                zz = lax.rem(z - s + nz, nz)
                for r in range(nr):
                    cols = pl.ds(pl.multiple_of(((zz * nr + r) * 4 + part) * bs, bs), bs)
                    v = tok[rows, cols].astype(F32) * inv * gain[:, cols]
                    out[rows, pl.ds((s * nr + r) * bs, bs)] = v.astype(BF16)


def normalise(tokens, gain, nz, nr, bs):
    rows, width = tokens.shape
    block = 32
    quarter = width // 4
    return pl.pallas_call(
        functools.partial(norm_kernel, nz=nz, nr=nr, bs=bs),
        grid=(rows // block,),
        in_specs=[pl.BlockSpec((block, width), lambda i: (i, 0)), pl.BlockSpec((1, width), lambda i: (0, 0))],
        out_specs=[pl.BlockSpec((block, quarter), lambda i: (i, 0))] * 4,
        out_shape=[jax.ShapeDtypeStruct((rows, quarter), BF16)] * 4,
        compiler_params=params(),
        cost_estimate=pl.CostEstimate(flops=8 * rows * width, bytes_accessed=4 * rows * width, transcendentals=0),
        name="norm",
    )(tokens, gain.reshape(1, width))


def project_kernel(*refs, halves):
    toks, refs = refs[:4], refs[4:]
    count = sum(pieces for _, _, pieces in halves)
    weights, refs = list(refs[:count]), refs[count:]
    (mine, core, square), (tbuf, wbuf, tsem, wsem) = refs[:3], refs[3:]
    outs = (mine, core.at[0], square, core.at[1])
    y = lax.axis_index("y")
    rows = mine.shape[0]
    steps, both, width = wbuf.shape
    half = both // 2
    tcopies, wcopies = [], [[] for _ in range(steps)]
    for step in range(steps):
        cols = pl.ds(step * both, both)
        tcopies.append(
            [
                pltpu.make_async_copy(
                    toks[i].at[:, cols], tbuf.at[pl.ds(i * rows, rows), cols], tsem.at[step, i]
                )
                for i in range(4)
            ]
        )
    for n, (step, far, pieces) in enumerate(halves):
        if far is None:
            span = pl.ds(0, both)
        else:
            span = pl.ds(pl.multiple_of((1 - y if far else y) * half, half), half)
        for j in range(pieces):
            size = width // pieces
            to = wbuf.at[step, span, pl.ds(j * size, size)]
            wcopies[step].append(pltpu.make_async_copy(weights.pop(0), to, wsem.at[n, j]))
    for step in range(steps):
        for cp in tcopies[step] + wcopies[step]:
            cp.start()
    for step in range(steps):
        for cp in tcopies[step] + wcopies[step]:
            cp.wait()
        v = jnp.dot(tbuf[:, step * both : (step + 1) * both], wbuf[step], preferred_element_type=F32)
        for i in range(4):
            part = v[i * rows : (i + 1) * rows]
            if step:
                outs[i][...] += part
            else:
                outs[i][...] = part


def project(toks, weights, halves):
    rows, depth = toks[0].shape
    steps = 1 + max(step for step, _, _ in halves)
    both = depth // steps
    width = sum(w.shape[1] for w in weights[0])
    anywhere = pl.BlockSpec(memory_space=pl.ANY)
    vmem = pl.BlockSpec(memory_space=pltpu.VMEM)
    flat = [w for pair in weights for w in pair]
    shapes = [(rows, width), (2, rows, width), (rows, width)]
    return pl.pallas_call(
        functools.partial(project_kernel, halves=halves),
        in_specs=[anywhere] * (4 + len(flat)),
        out_specs=[vmem] * 3,
        out_shape=[jax.ShapeDtypeStruct(shape, F32) for shape in shapes],
        scratch_shapes=[
            pltpu.VMEM((4 * rows, depth), BF16),
            pltpu.VMEM((steps, both, width), BF16),
            pltpu.SemaphoreType.DMA((steps, 4)),
            pltpu.SemaphoreType.DMA((len(halves), 2)),
        ],
        compiler_params=params(),
        cost_estimate=pl.CostEstimate(
            flops=2 * 4 * rows * depth * width, bytes_accessed=20 * 1024 * 1024, transcendentals=0
        ),
        name="project",
    )(*toks, *flat)


def prompt_index(nr):
    z, r, x, c = (lax.axis_index(a) for a in ("z", "r", "x", "c"))
    return ((z * nr + r) * 2 + x) * 2 + c


def attend_kernel(lens, mine, core, other, cos, sin, cache, out, kvbuf, sem, *, heads, head, nr):
    length = lens[prompt_index(nr)]
    slots = kvbuf.shape[0]
    rows = mine.shape[0]
    chunk = 1024
    copies = [
        pltpu.make_async_copy(
            cache.at[0, pl.ds(i * chunk, chunk)], kvbuf.at[pl.ds(i * chunk, chunk)], sem.at[i]
        )
        for i in range(slots // chunk)
    ]
    for cp in copies:
        cp.start()
    total = (mine[...] + core[0]) + other[...]

    def turn(v):
        return (v * cos[...] + pltpu.roll(v, head // 2, 1) * sin[...]).astype(BF16)

    q = jnp.concatenate([turn(total[:, i * head : (i + 1) * head]) for i in range(heads)], axis=0)
    k_new = turn(total[:, heads * head : (heads + 1) * head])
    v_new = total[:, (heads + 1) * head :].astype(BF16)
    scale = (head ** -0.5) * 1.4426950408889634

    def scores(keys):
        return lax.dot_general(q, keys, (((1,), (1,)), ((), ())), preferred_element_type=F32)

    s = scores(k_new)
    row = lax.broadcasted_iota(jnp.int32, s.shape, 0) % rows
    col = lax.broadcasted_iota(jnp.int32, s.shape, 1)
    s = jnp.where(col <= row, s, -1e30)
    top = jnp.max(s, axis=1, keepdims=True)
    p = jnp.exp2((s - top) * scale)
    total_p = jnp.sum(p, axis=1, keepdims=True)
    acc = jnp.dot(p.astype(BF16), v_new, preferred_element_type=F32)
    for i, cp in enumerate(copies):
        cp.wait()
        s = scores(kvbuf[pl.ds(i * chunk, chunk), :head])
        col = lax.broadcasted_iota(jnp.int32, (1, chunk), 1) + i * chunk
        s = jnp.where(col < length, s, -1e30)
        new_top = jnp.maximum(top, jnp.max(s, axis=1, keepdims=True))
        p = jnp.exp2((s - new_top) * scale)
        fade = jnp.exp2((top - new_top) * scale)
        top = new_top
        total_p = total_p * fade + jnp.sum(p, axis=1, keepdims=True)
        acc = acc * fade + jnp.dot(
            p.astype(BF16), kvbuf[pl.ds(i * chunk, chunk), head:], preferred_element_type=F32
        )
    acc = (acc / total_p).astype(BF16)
    for i in range(heads):
        out[:, i * head : (i + 1) * head] = acc[i * rows : (i + 1) * rows]


def attend(lens, mine, core, other, cos, sin, cache, heads, head, nr):
    vmem = pl.BlockSpec(memory_space=pltpu.VMEM)
    rows = mine.shape[0]
    slots = cache.shape[1]
    return pl.pallas_call(
        functools.partial(attend_kernel, heads=heads, head=head, nr=nr),
        in_specs=[pl.BlockSpec(memory_space=pltpu.SMEM)] + [vmem] * 5 + [pl.BlockSpec(memory_space=pl.ANY)],
        out_specs=vmem,
        out_shape=jax.ShapeDtypeStruct((rows, heads * head), BF16),
        scratch_shapes=[pltpu.VMEM(cache.shape[1:], BF16), pltpu.SemaphoreType.DMA((slots // 1024,))],
        compiler_params=params(),
        cost_estimate=pl.CostEstimate(
            flops=4 * rows * heads * head * slots, bytes_accessed=28 * 1024 * 1024, transcendentals=rows * heads * slots
        ),
        name="attend",
    )(lens, mine, core, other, cos, sin, cache)


def out_kernel(att, tok, *refs, plan, nz, nr, bs, carry):
    n = len(refs) - 6 - 1 - carry
    weights, out = refs[:n], refs[n + carry]
    refs = refs[carry:]
    wbuf, tbuf, obuf, wsem, tsem, osem = refs[n + 1 :]
    z, x, c, y = (lax.axis_index(a) for a in ("z", "x", "c", "y"))
    half = att.shape[1] // 2
    rows = att.shape[0]
    flip = y == 1
    low, high = att[:, :half], att[:, half:]
    left = jnp.concatenate([jnp.where(flip, high, low), jnp.where(flip, low, high)], axis=1)
    slots = wbuf.shape[0]

    def cols(s, dx, dc, r):
        zz = lax.rem(z - s + nz, nz)
        return pl.ds(pl.multiple_of(((zz * nr + r) * 4 + (x ^ dx) * 2 + (c ^ dc)) * bs, bs), bs)

    def load(b):
        (s, dx, dc), halves = plan[b]
        slot = b % slots
        cps = []
        for h, (ref, lead, pos) in enumerate(halves):
            src = weights[ref] if lead is None else weights[ref].at[lead]
            if pos is not None:
                side = y if pos == 0 else 1 - y
                src = src.at[pl.ds(pl.multiple_of(side * half, half), half)]
            cps.append(pltpu.make_async_copy(src, wbuf.at[slot, pl.ds(h * half, half)], wsem.at[slot, h]))
        for r in range(nr):
            cps.append(
                pltpu.make_async_copy(tok.at[:, cols(s, dx, dc, r)], tbuf.at[slot, :, pl.ds(r * bs, bs)], tsem.at[slot, r])
            )
        return cps

    def store(b):
        (s, dx, dc), _ = plan[b]
        slot = b % slots
        return [
            pltpu.make_async_copy(obuf.at[slot, :, pl.ds(r * bs, bs)], out.at[:, cols(s, dx, dc, r)], osem.at[slot, r])
            for r in range(nr)
        ]

    for b in range(min(slots, len(plan))):
        for cp in load(b):
            cp.start()
    for b in range(len(plan)):
        slot = b % slots
        for cp in load(b):
            cp.wait()
        if b >= slots:
            for cp in store(b - slots):
                cp.wait()
        v = jnp.dot(left, wbuf[slot], preferred_element_type=F32)
        obuf[slot] = (tbuf[slot].astype(F32) + v).astype(BF16)
        for cp in store(b):
            cp.start()
        if b + slots < len(plan):
            for cp in load(b + slots):
                cp.start()
    for b in range(max(0, len(plan) - slots), len(plan)):
        for cp in store(b):
            cp.wait()


def output(att, tokens, weights, plan, nz, nr, bs, base=None):
    anywhere = pl.BlockSpec(memory_space=pl.ANY)
    slots = 6
    rows, width = tokens.shape
    return pl.pallas_call(
        functools.partial(out_kernel, plan=plan, nz=nz, nr=nr, bs=bs, carry=int(base is not None)),
        in_specs=[pl.BlockSpec(memory_space=pltpu.VMEM)]
        + [anywhere] * (1 + len(weights) + (base is not None)),
        input_output_aliases={} if base is None else {2 + len(weights): 0},
        out_specs=anywhere,
        out_shape=jax.ShapeDtypeStruct(tokens.shape, BF16),
        scratch_shapes=[
            pltpu.VMEM((slots, att.shape[1], nr * bs), BF16),
            pltpu.VMEM((slots, rows, nr * bs), BF16),
            pltpu.VMEM((slots, rows, nr * bs), BF16),
            pltpu.SemaphoreType.DMA((slots, 2)),
            pltpu.SemaphoreType.DMA((slots, nr)),
            pltpu.SemaphoreType.DMA((slots, nr)),
        ],
        compiler_params=params(),
        cost_estimate=pl.CostEstimate(
            flops=2 * rows * nr * bs * len(plan) * att.shape[1],
            bytes_accessed=(att.shape[1] + 2 * rows) * 2 * nr * bs * len(plan),
            transcendentals=0,
        ),
        name="output",
    )(att, tokens, *weights, *(() if base is None else (base,)))


def body(tokens, gain, w_query, w_key_value, w_out, cache_kv, cached_len, *, nz, nr):
    rows = tokens.shape[0]
    head = w_key_value.shape[1] // 2
    heads = w_query.shape[1] // head
    bs = w_query.shape[0]
    y = lax.axis_index("y")
    length = jnp.sum(
        jnp.where(jnp.arange(cached_len.shape[0], dtype=jnp.int32) == prompt_index(nr), cached_len, 0)
    )

    def swap(v, axis):
        return lax.ppermute(v, axis, [(0, 1), (1, 0)])

    def ring(v):
        return lax.ppermute(v, "z", [(i, (i + 1) % nz) for i in range(nz)])

    own_q, own_kv, own_o = w_query, w_key_value, w_out
    if nr > 1:
        own_q = lax.all_gather(own_q, "r", axis=0, tiled=True)
        own_kv = lax.all_gather(own_kv, "r", axis=0, tiled=True)
        own_o = lax.all_gather(own_o, "r", axis=1, tiled=True)
    half = own_q.shape[0] // 2
    ohalf = own_o.shape[0] // 2

    def tie(v, *after):
        return lax.optimization_barrier((v,) + after)[0]

    w_mine = jnp.concatenate([lax.dynamic_slice_in_dim(w, y * half, half) for w in (own_q, own_kv)], axis=1)
    o_mine = lax.dynamic_slice_in_dim(own_o, y * ohalf, ohalf)
    o_else = lax.dynamic_slice_in_dim(own_o, (1 - y) * ohalf, ohalf)
    gain = tie(gain, w_mine, o_mine)
    with jax.named_scope("Ox"):
        o_mine_x = swap(o_mine, "x")
    toks = normalise(tokens, gain, nz, nr, bs)

    def step_z(v, name, *after):
        with jax.named_scope("Z" + name):
            return ring(tie(v, *after) if after else v)

    def step_y(v, name, *after):
        with jax.named_scope("Y" + name):
            return swap(tie(v, *after) if after else v, "y")

    w_near, w_far = [None], [None]
    with jax.named_scope("Tc"):
        core_toks = swap(toks[1], "c")
    with jax.named_scope("Tx"):
        across = swap(tie(toks[2], o_mine_x), "x")
    with jax.named_scope("Txc"):
        corner = lax.ppermute(toks[3], ("x", "c"), [(i, i ^ 3) for i in range(4)])
    with jax.named_scope("Oc0"):
        own_o_c = swap(own_o, "c")
        o_mine_x_c = swap(o_mine_x, "c")
    v = w_mine
    for s in range(1, nz):
        after = [w_far[s - 2], core_toks, across, own_o_c, o_mine_x_c] if s == 3 else []
        v = step_z(v, f"w{s}", *after)
        w_near.append(v)
        w_far.append(step_y(v, f"w{s}", *(w_far[2:] if s == 3 else [])))

    def weights_of(steps):
        weights, halves = [], []
        for s in steps:
            if s == 0:
                weights.append((own_q, own_kv))
                halves.append((0, None, 2))
                continue
            for side, held in enumerate((w_near, w_far)):
                weights.append((held[s],))
                halves.append((s - steps[0], side, 1))
        return weights, halves

    with jax.named_scope("Oxe"):
        o_else_x = swap(tie(o_else, w_near[3]), "x")
    o_near, o_far = [None], [None]
    o_near.append(step_z(jnp.stack([o_mine, tie(o_mine_x, toks[0])]), "o1", across))
    held = [toks[0], core_toks, across, tie(corner, o_near[1])]
    parts = project(held, *weights_of(range(nz)))
    o_near.append(step_z(o_near[1], "o2"))
    o_far.append(step_y(o_near[1], "o1"))
    with jax.named_scope("Pc"):
        from_c = swap(tie(parts[1], o_else_x), "c")
    total = parts[2] + tie(from_c, o_near[2], o_far[1])[1]
    with jax.named_scope("Px"):
        other = swap(total, "x")
    o_near.append(step_z(o_near[2], "o3", total))
    for s in range(2, nz):
        o_far.append(step_y(o_near[s], f"o{s}", total))
    with jax.named_scope("Oc1"):
        o_else_x_c = swap(tie(o_else_x, other), "c")
        near1_c = swap(tie(o_near[1], other), "c")
        far1_c = swap(tie(o_far[1], other), "c")

    positions = length.astype(F32) + jnp.arange(rows, dtype=F32)
    steps = jnp.arange(head // 2, dtype=F32) * (2.0 / head)
    freqs = jnp.exp(-jnp.log(jnp.float32(500000.0)) * steps)
    angles = positions[:, None] * freqs[None, :]
    cos, sin = jnp.cos(angles), jnp.sin(angles)
    att = attend(
        cached_len,
        parts[0],
        from_c,
        tie(other, o_near[3], o_far[2]),
        jnp.concatenate([cos, cos], axis=1),
        jnp.concatenate([-sin, sin], axis=1),
        cache_kv,
        heads,
        head,
        nr,
    )

    def over(v, dc, *after):
        if not dc:
            return v
        with jax.named_scope("Oc"):
            return swap(tie(v, *after), "c")

    def group(entries):
        weights, plan = [], []
        for place, halves in entries:
            spots = []
            for v, lead, pos in halves:
                at = [i for i, w in enumerate(weights) if w is v]
                if not at:
                    weights.append(v)
                    at = [len(weights) - 1]
                spots.append((at[0], lead, pos))
            plan.append((place, spots))
        return weights, plan

    def blocks(s, dc, near, far):
        return [((s, dx, dc), [(near, dx, None), (far, dx, None)]) for dx in range(2)]

    early, late = [], []
    for dc in range(2):
        own, mx, ex = ((own_o, o_mine_x, o_else_x), (own_o_c, o_mine_x_c, o_else_x_c))[dc]
        early.append(((0, 0, dc), [(own, None, 0), (own, None, 1)]))
        early.append(((0, 1, dc), [(mx, None, None), (ex, None, None)]))
    early += blocks(1, 0, o_near[1], o_far[1]) + blocks(1, 1, near1_c, far1_c) + blocks(2, 0, o_near[2], o_far[2])
    out = output(att, tokens, *group(early), nz, nr, bs)
    late += blocks(2, 1, over(o_near[2], 1, att), over(o_far[2], 1, att))
    for dc in range(2):
        late += blocks(3, dc, over(o_near[3], dc, att), over(o_far[3], dc, out))
    return output(att, tokens, *group(late), nz, nr, bs, out)


def solution(mesh):
    groups, blk = mesh.shape["groups"], mesh.shape["blk"]
    nz = 4
    nr = blk // (4 * nz)
    wide = Mesh(mesh.devices.reshape(groups, nz, nr, 2, 2), AXES)
    blocks = ("z", "r", "x", "c")
    placed = (
        P(AXES, None),
        P(),
        P(blocks, None),
        P(blocks, None),
        P(None, blocks),
        P(AXES, None, None),
        P("y"),
    )
    return jax.shard_map(
        functools.partial(body, nz=nz, nr=nr),
        mesh=wide,
        in_specs=placed,
        out_specs=P(AXES, None),
        check_vma=False,
    )
```

```python
import functools
import math

import jax
import jax.numpy as jnp
from jax import lax
from jax.experimental import pallas as pl
from jax.experimental.pallas import tpu as pltpu
from jax.sharding import Mesh, PartitionSpec as P

F32 = jnp.float32
BF16 = jnp.bfloat16
AXES = ("y", "z", "r", "x", "c")


def params(mib):
    return pltpu.CompilerParams(vmem_limit_bytes=mib * 1024 * 1024)


def gather_kernel(*refs, jobs):
    y = lax.axis_index("y")
    sem = refs[-1]
    copies = []
    for i, (src, side, rows, dst, lead, cols) in enumerate(jobs):
        ref, to = refs[src], refs[dst]
        if side is not None:
            ref = ref.at[pl.ds(pl.multiple_of((y if side == 0 else 1 - y) * rows, rows), rows)]
        if lead is not None:
            to = to.at[lead]
        if cols is not None:
            to = to.at[:, pl.ds(*cols)]
        copies.append(pltpu.make_async_copy(ref, to, sem.at[i]))
    for cp in copies:
        cp.start()
    for cp in copies:
        cp.wait()


def gather(arrays, shapes, jobs, name, limit, space):
    anywhere = pl.BlockSpec(memory_space=pl.ANY)
    size = sum(math.prod(shape) for shape in shapes)
    return pl.pallas_call(
        functools.partial(gather_kernel, jobs=jobs),
        in_specs=[anywhere] * len(arrays),
        out_specs=[pl.BlockSpec(memory_space=space)] * len(shapes),
        out_shape=[jax.ShapeDtypeStruct(shape, BF16) for shape in shapes],
        scratch_shapes=[pltpu.SemaphoreType.DMA((len(jobs),))],
        compiler_params=params(limit),
        cost_estimate=pl.CostEstimate(flops=0, bytes_accessed=4 * size, transcendentals=0),
        name=name,
    )(*arrays)


def norm_kernel(tokens, gain, *refs, nz, nr, bs, block):
    z, x, c = (lax.axis_index(a) for a in ("z", "x", "c"))
    outs, tbuf, sem = refs[:4], refs[4], refs[5]
    n = pl.program_id(0)

    def load(i):
        return pltpu.make_async_copy(tokens.at[pl.ds(i * block, block)], tbuf.at[i], sem.at[i])

    @pl.when(n == 0)
    def _():
        for i in range(tbuf.shape[0]):
            load(i).start()

    load(n).wait()
    tok = tbuf.at[n]
    width = tok.shape[1]
    step = 1024
    for r0 in range(0, block, 16):
        rows = pl.ds(r0, 16)
        acc = jnp.zeros((16, step), F32)
        for j in range(width // step):
            v = tok[rows, pl.ds(j * step, step)].astype(F32)
            acc = acc + v * v
        inv = lax.rsqrt(jnp.sum(acc, axis=1, keepdims=True) * (1.0 / width) + 1e-05)
        for k, out in enumerate(outs):
            part = (x ^ (k // 2)) * 2 + (c ^ (k % 2))
            for s in range(nz):
                zz = lax.rem(z - s + nz, nz)
                for r in range(nr):
                    cols = pl.ds(pl.multiple_of(((zz * nr + r) * 4 + part) * bs, bs), bs)
                    v = tok[rows, cols].astype(F32) * inv * gain[:, cols]
                    out[rows, pl.ds((s * nr + r) * bs, bs)] = v.astype(BF16)


def normalise(tokens, gain, nz, nr, bs):
    rows, width = tokens.shape
    block = 32
    quarter = width // 4
    return pl.pallas_call(
        functools.partial(norm_kernel, nz=nz, nr=nr, bs=bs, block=block),
        grid=(rows // block,),
        in_specs=[pl.BlockSpec(memory_space=pl.ANY), pl.BlockSpec((1, width), lambda i: (0, 0))],
        out_specs=[pl.BlockSpec((block, quarter), lambda i: (i, 0))] * 4,
        out_shape=[jax.ShapeDtypeStruct((rows, quarter), BF16)] * 4,
        scratch_shapes=[pltpu.VMEM((rows // block, block, width), BF16), pltpu.SemaphoreType.DMA((rows // block,))],
        compiler_params=params(56),
        cost_estimate=pl.CostEstimate(flops=8 * rows * width, bytes_accessed=rows * width, transcendentals=0),
        name="norm",
    )(tokens, gain.reshape(1, width))


def project_kernel(*refs, halves):
    toks, refs = refs[:4], refs[4:]
    count = sum(pieces for _, _, pieces in halves)
    weights, refs = list(refs[:count]), refs[count:]
    (mine, core, square), (tbuf, wbuf, tsem, wsem) = refs[:3], refs[3:]
    outs = (mine, core.at[0], square, core.at[1])
    y = lax.axis_index("y")
    rows = mine.shape[0]
    steps, both, width = wbuf.shape
    half = both // 2
    tcopies, wcopies = [], [[] for _ in range(steps)]
    for step in range(steps):
        cols = pl.ds(step * both, both)
        tcopies.append(
            [
                pltpu.make_async_copy(
                    toks[i].at[:, cols], tbuf.at[pl.ds(i * rows, rows), cols], tsem.at[step, i]
                )
                for i in range(4)
            ]
        )
    for n, (step, far, pieces) in enumerate(halves):
        if far is None:
            span = pl.ds(0, both)
        else:
            span = pl.ds(pl.multiple_of((1 - y if far else y) * half, half), half)
        for j in range(pieces):
            size = width // pieces
            to = wbuf.at[step, span, pl.ds(j * size, size)]
            wcopies[step].append(pltpu.make_async_copy(weights.pop(0), to, wsem.at[n, j]))
    for step in range(steps):
        for cp in tcopies[step] + wcopies[step]:
            cp.start()
    for step in range(steps):
        for cp in tcopies[step] + wcopies[step]:
            cp.wait()
        v = jnp.dot(tbuf[:, step * both : (step + 1) * both], wbuf[step], preferred_element_type=F32)
        for i in range(4):
            part = v[i * rows : (i + 1) * rows]
            if step:
                outs[i][...] += part
            else:
                outs[i][...] = part


def project(toks, weights, halves):
    rows, depth = toks[0].shape
    steps = 1 + max(step for step, _, _ in halves)
    both = depth // steps
    width = sum(w.shape[1] for w in weights[0])
    anywhere = pl.BlockSpec(memory_space=pl.ANY)
    vmem = pl.BlockSpec(memory_space=pltpu.VMEM)
    flat = [w for pair in weights for w in pair]
    shapes = [(rows, width), (2, rows, width), (rows, width)]
    return pl.pallas_call(
        functools.partial(project_kernel, halves=halves),
        in_specs=[anywhere] * (4 + len(flat)),
        out_specs=[vmem] * 3,
        out_shape=[jax.ShapeDtypeStruct(shape, F32) for shape in shapes],
        scratch_shapes=[
            pltpu.VMEM((4 * rows, depth), BF16),
            pltpu.VMEM((steps, both, width), BF16),
            pltpu.SemaphoreType.DMA((steps, 4)),
            pltpu.SemaphoreType.DMA((len(halves), 2)),
        ],
        compiler_params=params(16),
        cost_estimate=pl.CostEstimate(
            flops=2 * 4 * rows * depth * width, bytes_accessed=2 * 1024 * 1024, transcendentals=0
        ),
        name="project",
    )(*toks, *flat)


def prompt_index(nr):
    z, r, x, c = (lax.axis_index(a) for a in ("z", "r", "x", "c"))
    return ((z * nr + r) * 2 + x) * 2 + c


def attend_kernel(lens, *refs, heads, head, nr):
    mine, core, other, turns, cache, out, pbuf, kvbuf, psem, sem = refs
    length = lens[prompt_index(nr)]
    slots = kvbuf.shape[0]
    rows = mine.shape[0]
    chunk = 1024
    copies = [
        pltpu.make_async_copy(
            cache.at[0, pl.ds(i * chunk, chunk)], kvbuf.at[pl.ds(i * chunk, chunk)], sem.at[i]
        )
        for i in range(slots // chunk)
    ]
    sums = [
        pltpu.make_async_copy(ref, pbuf.at[i], psem.at[i]) for i, ref in enumerate((mine, core.at[0], other))
    ]
    for cp in sums + copies:
        cp.start()
    for cp in sums:
        cp.wait()
    total = (pbuf[0] + pbuf[1]) + pbuf[2]

    def turn(v):
        return (v * turns[0] + pltpu.roll(v, head // 2, 1) * turns[1]).astype(BF16)

    q = jnp.concatenate([turn(total[:, i * head : (i + 1) * head]) for i in range(heads)], axis=0)
    k_new = turn(total[:, heads * head : (heads + 1) * head])
    v_new = total[:, (heads + 1) * head :].astype(BF16)
    scale = (head ** -0.5) * 1.4426950408889634

    def scores(keys):
        return lax.dot_general(q, keys, (((1,), (1,)), ((), ())), preferred_element_type=F32)

    s = scores(k_new)
    row = lax.broadcasted_iota(jnp.int32, s.shape, 0) % rows
    col = lax.broadcasted_iota(jnp.int32, s.shape, 1)
    s = jnp.where(col <= row, s, -1e30)
    top = jnp.max(s, axis=1, keepdims=True)
    p = jnp.exp2((s - top) * scale)
    total_p = jnp.sum(p, axis=1, keepdims=True)
    acc = jnp.dot(p.astype(BF16), v_new, preferred_element_type=F32)
    for i, cp in enumerate(copies):
        cp.wait()
        s = scores(kvbuf[pl.ds(i * chunk, chunk), :head])
        col = lax.broadcasted_iota(jnp.int32, (1, chunk), 1) + i * chunk
        s = jnp.where(col < length, s, -1e30)
        new_top = jnp.maximum(top, jnp.max(s, axis=1, keepdims=True))
        p = jnp.exp2((s - new_top) * scale)
        fade = jnp.exp2((top - new_top) * scale)
        top = new_top
        total_p = total_p * fade + jnp.sum(p, axis=1, keepdims=True)
        acc = acc * fade + jnp.dot(
            p.astype(BF16), kvbuf[pl.ds(i * chunk, chunk), head:], preferred_element_type=F32
        )
    acc = (acc / total_p).astype(BF16)
    for i in range(heads):
        out[:, i * head : (i + 1) * head] = acc[i * rows : (i + 1) * rows]


def attend(lens, mine, core, other, turns, cache, heads, head, nr):
    vmem = pl.BlockSpec(memory_space=pltpu.VMEM)
    rows = mine.shape[0]
    slots = cache.shape[1]
    anywhere = pl.BlockSpec(memory_space=pl.ANY)
    return pl.pallas_call(
        functools.partial(attend_kernel, heads=heads, head=head, nr=nr),
        in_specs=[pl.BlockSpec(memory_space=pltpu.SMEM)] + [anywhere] * 3 + [vmem, anywhere],
        out_specs=vmem,
        out_shape=jax.ShapeDtypeStruct((rows, heads * head), BF16),
        scratch_shapes=[
            pltpu.VMEM((3,) + mine.shape, F32),
            pltpu.VMEM(cache.shape[1:], BF16),
            pltpu.SemaphoreType.DMA((3,)),
            pltpu.SemaphoreType.DMA((slots // 1024,)),
        ],
        compiler_params=params(20),
        cost_estimate=pl.CostEstimate(
            flops=4 * rows * heads * head * slots, bytes_accessed=28 * 1024 * 1024, transcendentals=rows * heads * slots
        ),
        name="attend",
    )(lens, mine, core, other, turns, cache)


def out_kernel(att, tok, *refs, plan, nz, nr, bs, carry):
    n = len(refs) - 6 - 1 - carry
    weights, out = refs[:n], refs[n + carry]
    refs = refs[carry:]
    wbuf, tbuf, obuf, wsem, tsem, osem = refs[n + 1 :]
    z, x, c, y = (lax.axis_index(a) for a in ("z", "x", "c", "y"))
    half = att.shape[1] // 2
    rows = att.shape[0]
    flip = y == 1
    low, high = att[:, :half], att[:, half:]
    left = jnp.concatenate([jnp.where(flip, high, low), jnp.where(flip, low, high)], axis=1)
    slots = wbuf.shape[0]

    def cols(s, dx, dc, r):
        zz = lax.rem(z - s + nz, nz)
        return pl.ds(pl.multiple_of(((zz * nr + r) * 4 + (x ^ dx) * 2 + (c ^ dc)) * bs, bs), bs)

    def load(b):
        (s, dx, dc), halves = plan[b]
        slot = b % slots
        cps = []
        for h, (ref, lead, pos) in enumerate(halves):
            src = weights[ref] if lead is None else weights[ref].at[lead]
            if pos is not None:
                side = y if pos == 0 else 1 - y
                src = src.at[pl.ds(pl.multiple_of(side * half, half), half)]
            cps.append(pltpu.make_async_copy(src, wbuf.at[slot, pl.ds(h * half, half)], wsem.at[slot, h]))
        for r in range(nr):
            cps.append(
                pltpu.make_async_copy(tok.at[:, cols(s, dx, dc, r)], tbuf.at[slot, :, pl.ds(r * bs, bs)], tsem.at[slot, r])
            )
        return cps

    def store(b):
        (s, dx, dc), _ = plan[b]
        slot = b % slots
        return [
            pltpu.make_async_copy(obuf.at[slot, :, pl.ds(r * bs, bs)], out.at[:, cols(s, dx, dc, r)], osem.at[slot, r])
            for r in range(nr)
        ]

    for b in range(min(slots, len(plan))):
        for cp in load(b):
            cp.start()
    for b in range(len(plan)):
        slot = b % slots
        for cp in load(b):
            cp.wait()
        if b >= slots:
            for cp in store(b - slots):
                cp.wait()
        v = jnp.dot(left, wbuf[slot], preferred_element_type=F32)
        obuf[slot] = (tbuf[slot].astype(F32) + v).astype(BF16)
        for cp in store(b):
            cp.start()
        if b + slots < len(plan):
            for cp in load(b + slots):
                cp.start()
    for b in range(max(0, len(plan) - slots), len(plan)):
        for cp in store(b):
            cp.wait()


def output(att, tokens, weights, plan, nz, nr, bs, base=None):
    anywhere = pl.BlockSpec(memory_space=pl.ANY)
    slots = 6
    rows, width = tokens.shape
    return pl.pallas_call(
        functools.partial(out_kernel, plan=plan, nz=nz, nr=nr, bs=bs, carry=int(base is not None)),
        in_specs=[pl.BlockSpec(memory_space=pltpu.VMEM)]
        + [anywhere] * (1 + len(weights) + (base is not None)),
        input_output_aliases={} if base is None else {2 + len(weights): 0},
        out_specs=anywhere,
        out_shape=jax.ShapeDtypeStruct(tokens.shape, BF16),
        scratch_shapes=[
            pltpu.VMEM((slots, att.shape[1], nr * bs), BF16),
            pltpu.VMEM((slots, rows, nr * bs), BF16),
            pltpu.VMEM((slots, rows, nr * bs), BF16),
            pltpu.SemaphoreType.DMA((slots, 2)),
            pltpu.SemaphoreType.DMA((slots, nr)),
            pltpu.SemaphoreType.DMA((slots, nr)),
        ],
        compiler_params=params(12),
        cost_estimate=pl.CostEstimate(
            flops=2 * rows * nr * bs * len(plan) * att.shape[1],
            bytes_accessed=(att.shape[1] + 2 * rows) * 2 * nr * bs * len(plan),
            transcendentals=0,
        ),
        name="output",
    )(att, tokens, *weights, *(() if base is None else (base,)))


def trig(lens, rows, head, nr):
    length = jnp.sum(jnp.where(jnp.arange(lens.shape[0], dtype=jnp.int32) == prompt_index(nr), lens, 0))
    positions = length.astype(F32) + jnp.arange(rows, dtype=F32)
    steps = jnp.arange(head // 2, dtype=F32) * (2.0 / head)
    freqs = jnp.exp(-jnp.log(jnp.float32(500000.0)) * steps)
    angles = positions[:, None] * freqs[None, :]
    cos, sin = jnp.cos(angles), jnp.sin(angles)
    return jnp.stack([jnp.concatenate([cos, cos], axis=1), jnp.concatenate([-sin, sin], axis=1)])


def body(tokens, gain, w_query, w_key_value, w_out, cache_kv, cached_len, *, nz, nr):
    rows = tokens.shape[0]
    head = w_key_value.shape[1] // 2
    heads = w_query.shape[1] // head
    bs = w_query.shape[0]
    y = lax.axis_index("y")
    def swap(v, axis):
        return lax.ppermute(v, axis, [(0, 1), (1, 0)])

    def ring(v):
        return lax.ppermute(v, "z", [(i, (i + 1) % nz) for i in range(nz)])

    own_q, own_kv, own_o = w_query, w_key_value, w_out
    if nr > 1:
        own_q = lax.all_gather(own_q, "r", axis=0, tiled=True)
        own_kv = lax.all_gather(own_kv, "r", axis=0, tiled=True)
        own_o = lax.all_gather(own_o, "r", axis=1, tiled=True)
    half = own_q.shape[0] // 2
    ohalf = own_o.shape[0] // 2

    def tie(v, *after):
        return lax.optimization_barrier((v,) + after)[0]

    width = own_q.shape[1]
    with jax.named_scope("Ox"):
        x_o = swap(own_o, "x")
    (w_mine,) = gather(
        (own_q, own_kv),
        ((half, 2 * width),),
        ((0, 0, half, 2, None, (0, width)), (1, 0, half, 2, None, (width, width))),
        "pick",
        56,
        pltpu.VMEM,
    )
    toks = normalise(tokens, tie(gain, w_mine), nz, nr, bs)

    def step_z(v, name, *after):
        with jax.named_scope("Z" + name):
            return ring(tie(v, *after) if after else v)

    def step_y(v, name, *after):
        with jax.named_scope("Y" + name):
            return swap(tie(v, *after) if after else v, "y")

    w_near, w_far = [None], [None]
    with jax.named_scope("Tc"):
        core_toks = swap(toks[1], "c")
    with jax.named_scope("Tx"):
        across = swap(toks[2], "x")
    with jax.named_scope("Txc"):
        corner = lax.ppermute(toks[3], ("x", "c"), [(i, i ^ 3) for i in range(4)])
    with jax.named_scope("Oc0"):
        own_o_c = swap(own_o, "c")
        x_o_c = swap(x_o, "c")
    (pair,) = gather(
        (own_o, x_o),
        ((2, ohalf, own_o.shape[1]),),
        ((0, 0, ohalf, 2, 0, None), (1, 0, ohalf, 2, 1, None)),
        "pair",
        4,
        pltpu.VMEM,
    )
    v = w_mine
    turns = None
    for s in range(1, nz):
        if s == nz - 1:
            turns = trig(tie(cached_len, w_near[1]), rows, head, nr)
        after = [w_far[s - 2], core_toks, own_o_c, x_o_c, turns] if s == 3 else []
        v = step_z(v, f"w{s}", *after)
        w_near.append(v)
        w_far.append(step_y(v, f"w{s}", *(w_far[2:] if s == 3 else [])))

    def weights_of(steps):
        weights, halves = [], []
        for s in steps:
            if s == 0:
                weights.append((own_q, own_kv))
                halves.append((0, None, 2))
                continue
            for side, held in enumerate((w_near, w_far)):
                weights.append((held[s],))
                halves.append((s - steps[0], side, 1))
        return weights, halves

    o_near, o_far = [None], [None]
    o_near.append(step_z(pair, "o1", across))
    held = [toks[0], core_toks, across, tie(corner, o_near[1])]
    parts = project(held, *weights_of(range(nz)))
    o_near.append(step_z(o_near[1], "o2"))
    o_far.append(step_y(o_near[1], "o1"))
    with jax.named_scope("Pc"):
        from_c = swap(tie(parts[1], o_near[2], o_far[1]), "c")
    total = parts[2] + from_c[1]
    with jax.named_scope("Px"):
        other = swap(total, "x")
    o_near.append(step_z(o_near[2], "o3"))
    for s in range(2, nz):
        o_far.append(step_y(o_near[s], f"o{s}"))
    with jax.named_scope("Oc1"):
        near1_c = swap(tie(o_near[1], other), "c")
        far1_c = swap(tie(o_far[1], other), "c")

    att = attend(
        cached_len,
        parts[0],
        from_c,
        tie(other, o_near[3]),
        turns,
        cache_kv,
        heads,
        head,
        nr,
    )

    def over(v, dc, *after):
        if not dc:
            return v
        with jax.named_scope("Oc"):
            return swap(tie(v, *after), "c")

    def group(entries):
        weights, plan = [], []
        for place, halves in entries:
            spots = []
            for v, lead, pos in halves:
                at = [i for i, w in enumerate(weights) if w is v]
                if not at:
                    weights.append(v)
                    at = [len(weights) - 1]
                spots.append((at[0], lead, pos))
            plan.append((place, spots))
        return weights, plan

    def blocks(s, dc, near, far):
        return [((s, dx, dc), [(near, dx, None), (far, dx, None)]) for dx in range(2)]

    early, late = [], []
    for dc in range(2):
        for dx, v in enumerate(((own_o, x_o), (own_o_c, x_o_c))[dc]):
            early.append(((0, dx, dc), [(v, None, 0), (v, None, 1)]))
    early += blocks(1, 0, o_near[1], o_far[1]) + blocks(1, 1, near1_c, far1_c) + blocks(2, 0, o_near[2], o_far[2])
    out = output(att, tokens, *group(early), nz, nr, bs)
    late += blocks(2, 1, over(o_near[2], 1, att), over(o_far[2], 1, att))
    for dc in range(2):
        late += blocks(3, dc, over(o_near[3], dc, att), over(o_far[3], dc, out))
    return output(att, tokens, *group(late), nz, nr, bs, out)


def solution(mesh):
    groups, blk = mesh.shape["groups"], mesh.shape["blk"]
    nz = 4
    nr = blk // (4 * nz)
    wide = Mesh(mesh.devices.reshape(groups, nz, nr, 2, 2), AXES)
    blocks = ("z", "r", "x", "c")
    placed = (
        P(AXES, None),
        P(),
        P(blocks, None),
        P(blocks, None),
        P(None, blocks),
        P(AXES, None, None),
        P("y"),
    )
    return jax.shard_map(
        functools.partial(body, nz=nz, nr=nr),
        mesh=wide,
        in_specs=placed,
        out_specs=P(AXES, None),
        check_vma=False,
    )
```

```python
import functools
import math

import jax
import jax.numpy as jnp
from jax import lax
from jax.experimental import pallas as pl
from jax.experimental.pallas import tpu as pltpu
from jax.sharding import Mesh, PartitionSpec as P

F32 = jnp.float32
BF16 = jnp.bfloat16
AXES = ("y", "z", "r", "x", "c")


def params(mib):
    return pltpu.CompilerParams(vmem_limit_bytes=mib * 1024 * 1024)


def gather_kernel(*refs, jobs):
    y = lax.axis_index("y")
    sem = refs[-1]
    copies = []
    for i, (src, side, rows, dst, lead, cols) in enumerate(jobs):
        ref, to = refs[src], refs[dst]
        if side is not None:
            ref = ref.at[pl.ds(pl.multiple_of((y if side == 0 else 1 - y) * rows, rows), rows)]
        if lead is not None:
            to = to.at[lead]
        if cols is not None:
            to = to.at[:, pl.ds(*cols)]
        copies.append(pltpu.make_async_copy(ref, to, sem.at[i]))
    for cp in copies:
        cp.start()
    for cp in copies:
        cp.wait()


def gather(arrays, shapes, jobs, name, limit, space):
    anywhere = pl.BlockSpec(memory_space=pl.ANY)
    size = sum(math.prod(shape) for shape in shapes)
    return pl.pallas_call(
        functools.partial(gather_kernel, jobs=jobs),
        in_specs=[anywhere] * len(arrays),
        out_specs=[pl.BlockSpec(memory_space=space)] * len(shapes),
        out_shape=[jax.ShapeDtypeStruct(shape, BF16) for shape in shapes],
        scratch_shapes=[pltpu.SemaphoreType.DMA((len(jobs),))],
        compiler_params=params(limit),
        cost_estimate=pl.CostEstimate(flops=0, bytes_accessed=4 * size, transcendentals=0),
        name=name,
    )(*arrays)


def norm_kernel(tokens, gain, *refs, nz, nr, bs, block):
    z, x, c = (lax.axis_index(a) for a in ("z", "x", "c"))
    outs, tbuf, sem = refs[:4], refs[4], refs[5]
    n = pl.program_id(0)

    def load(i):
        return pltpu.make_async_copy(tokens.at[pl.ds(i * block, block)], tbuf.at[i], sem.at[i])

    @pl.when(n == 0)
    def _():
        for i in range(tbuf.shape[0]):
            load(i).start()

    load(n).wait()
    tok = tbuf.at[n]
    width = tok.shape[1]
    step = 1024
    for r0 in range(0, block, 16):
        rows = pl.ds(r0, 16)
        acc = jnp.zeros((16, step), F32)
        for j in range(width // step):
            v = tok[rows, pl.ds(j * step, step)].astype(F32)
            acc = acc + v * v
        inv = lax.rsqrt(jnp.sum(acc, axis=1, keepdims=True) * (1.0 / width) + 1e-05)
        for k, out in enumerate(outs):
            part = (x ^ (k // 2)) * 2 + (c ^ (k % 2))
            for s in range(nz):
                zz = lax.rem(z - s + nz, nz)
                for r in range(nr):
                    cols = pl.ds(pl.multiple_of(((zz * nr + r) * 4 + part) * bs, bs), bs)
                    v = tok[rows, cols].astype(F32) * inv * gain[:, cols]
                    out[rows, pl.ds((s * nr + r) * bs, bs)] = v.astype(BF16)


def normalise(tokens, gain, nz, nr, bs):
    rows, width = tokens.shape
    block = 32
    quarter = width // 4
    return pl.pallas_call(
        functools.partial(norm_kernel, nz=nz, nr=nr, bs=bs, block=block),
        grid=(rows // block,),
        in_specs=[pl.BlockSpec(memory_space=pl.ANY), pl.BlockSpec((1, width), lambda i: (0, 0))],
        out_specs=[pl.BlockSpec((block, quarter), lambda i: (i, 0))] * 4,
        out_shape=[jax.ShapeDtypeStruct((rows, quarter), BF16)] * 4,
        scratch_shapes=[pltpu.VMEM((rows // block, block, width), BF16), pltpu.SemaphoreType.DMA((rows // block,))],
        compiler_params=params(56),
        cost_estimate=pl.CostEstimate(flops=8 * rows * width, bytes_accessed=rows * width, transcendentals=0),
        name="norm",
    )(tokens, gain.reshape(1, width))


def project_kernel(*refs, halves):
    toks, refs = refs[:4], refs[4:]
    count = sum(pieces for _, _, pieces in halves)
    weights, refs = list(refs[:count]), refs[count:]
    (mine, core, square), (tbuf, wbuf, tsem, wsem) = refs[:3], refs[3:]
    outs = (mine, core.at[0], square, core.at[1])
    y = lax.axis_index("y")
    rows = mine.shape[0]
    steps, both, width = wbuf.shape
    half = both // 2
    tcopies, wcopies = [], [[] for _ in range(steps)]
    for step in range(steps):
        cols = pl.ds(step * both, both)
        tcopies.append(
            [
                pltpu.make_async_copy(
                    toks[i].at[:, cols], tbuf.at[pl.ds(i * rows, rows), cols], tsem.at[step, i]
                )
                for i in range(4)
            ]
        )
    for n, (step, far, pieces) in enumerate(halves):
        if far is None:
            span = pl.ds(0, both)
        else:
            span = pl.ds(pl.multiple_of((1 - y if far else y) * half, half), half)
        for j in range(pieces):
            size = width // pieces
            to = wbuf.at[step, span, pl.ds(j * size, size)]
            wcopies[step].append(pltpu.make_async_copy(weights.pop(0), to, wsem.at[n, j]))
    for step in range(steps):
        for cp in tcopies[step] + wcopies[step]:
            cp.start()
    for step in range(steps):
        for cp in tcopies[step] + wcopies[step]:
            cp.wait()
        v = jnp.dot(tbuf[:, step * both : (step + 1) * both], wbuf[step], preferred_element_type=F32)
        for i in range(4):
            part = v[i * rows : (i + 1) * rows]
            if step:
                outs[i][...] += part
            else:
                outs[i][...] = part


def project(toks, weights, halves):
    rows, depth = toks[0].shape
    steps = 1 + max(step for step, _, _ in halves)
    both = depth // steps
    width = sum(w.shape[1] for w in weights[0])
    anywhere = pl.BlockSpec(memory_space=pl.ANY)
    vmem = pl.BlockSpec(memory_space=pltpu.VMEM)
    flat = [w for pair in weights for w in pair]
    shapes = [(rows, width), (2, rows, width), (rows, width)]
    return pl.pallas_call(
        functools.partial(project_kernel, halves=halves),
        in_specs=[anywhere] * (4 + len(flat)),
        out_specs=[vmem] * 3,
        out_shape=[jax.ShapeDtypeStruct(shape, F32) for shape in shapes],
        scratch_shapes=[
            pltpu.VMEM((4 * rows, depth), BF16),
            pltpu.VMEM((steps, both, width), BF16),
            pltpu.SemaphoreType.DMA((steps, 4)),
            pltpu.SemaphoreType.DMA((len(halves), 2)),
        ],
        compiler_params=params(16),
        cost_estimate=pl.CostEstimate(
            flops=2 * 4 * rows * depth * width, bytes_accessed=2 * 1024 * 1024, transcendentals=0
        ),
        name="project",
    )(*toks, *flat)


def prompt_index(nr):
    z, r, x, c = (lax.axis_index(a) for a in ("z", "r", "x", "c"))
    return ((z * nr + r) * 2 + x) * 2 + c


def attend_kernel(lens, *refs, heads, head, nr):
    mine, core, other, turns, cache, out, pbuf, kvbuf, psem, sem = refs
    length = lens[prompt_index(nr)]
    slots = kvbuf.shape[0]
    rows = mine.shape[0]
    chunk = 1024
    copies = [
        pltpu.make_async_copy(
            cache.at[0, pl.ds(i * chunk, chunk)], kvbuf.at[pl.ds(i * chunk, chunk)], sem.at[i]
        )
        for i in range(slots // chunk)
    ]
    sums = [
        pltpu.make_async_copy(ref, pbuf.at[i], psem.at[i]) for i, ref in enumerate((mine, core.at[0], other))
    ]
    for cp in sums + copies:
        cp.start()
    for cp in sums:
        cp.wait()
    total = (pbuf[0] + pbuf[1]) + pbuf[2]

    def turn(v):
        return (v * turns[0] + pltpu.roll(v, head // 2, 1) * turns[1]).astype(BF16)

    q = jnp.concatenate([turn(total[:, i * head : (i + 1) * head]) for i in range(heads)], axis=0)
    k_new = turn(total[:, heads * head : (heads + 1) * head])
    v_new = total[:, (heads + 1) * head :].astype(BF16)
    scale = (head ** -0.5) * 1.4426950408889634

    def scores(keys):
        return lax.dot_general(q, keys, (((1,), (1,)), ((), ())), preferred_element_type=F32)

    s = scores(k_new)
    row = lax.broadcasted_iota(jnp.int32, s.shape, 0) % rows
    col = lax.broadcasted_iota(jnp.int32, s.shape, 1)
    s = jnp.where(col <= row, s, -1e30)
    top = jnp.max(s, axis=1, keepdims=True)
    p = jnp.exp2((s - top) * scale)
    total_p = jnp.sum(p, axis=1, keepdims=True)
    acc = jnp.dot(p.astype(BF16), v_new, preferred_element_type=F32)
    for i, cp in enumerate(copies):
        cp.wait()
        s = scores(kvbuf[pl.ds(i * chunk, chunk), :head])
        col = lax.broadcasted_iota(jnp.int32, (1, chunk), 1) + i * chunk
        s = jnp.where(col < length, s, -1e30)
        new_top = jnp.maximum(top, jnp.max(s, axis=1, keepdims=True))
        p = jnp.exp2((s - new_top) * scale)
        fade = jnp.exp2((top - new_top) * scale)
        top = new_top
        total_p = total_p * fade + jnp.sum(p, axis=1, keepdims=True)
        acc = acc * fade + jnp.dot(
            p.astype(BF16), kvbuf[pl.ds(i * chunk, chunk), head:], preferred_element_type=F32
        )
    acc = (acc / total_p).astype(BF16)
    for i in range(heads):
        out[:, i * head : (i + 1) * head] = acc[i * rows : (i + 1) * rows]


def attend(lens, mine, core, other, turns, cache, heads, head, nr):
    vmem = pl.BlockSpec(memory_space=pltpu.VMEM)
    rows = mine.shape[0]
    slots = cache.shape[1]
    anywhere = pl.BlockSpec(memory_space=pl.ANY)
    return pl.pallas_call(
        functools.partial(attend_kernel, heads=heads, head=head, nr=nr),
        in_specs=[pl.BlockSpec(memory_space=pltpu.SMEM)] + [anywhere] * 3 + [vmem, anywhere],
        out_specs=vmem,
        out_shape=jax.ShapeDtypeStruct((rows, heads * head), BF16),
        scratch_shapes=[
            pltpu.VMEM((3,) + mine.shape, F32),
            pltpu.VMEM(cache.shape[1:], BF16),
            pltpu.SemaphoreType.DMA((3,)),
            pltpu.SemaphoreType.DMA((slots // 1024,)),
        ],
        compiler_params=params(20),
        cost_estimate=pl.CostEstimate(
            flops=4 * rows * heads * head * slots, bytes_accessed=28 * 1024 * 1024, transcendentals=rows * heads * slots
        ),
        name="attend",
    )(lens, mine, core, other, turns, cache)


def out_kernel(att, tok, *refs, plan, nz, nr, bs, carry):
    n = len(refs) - 6 - 1 - carry
    weights, out = refs[:n], refs[n + carry]
    refs = refs[carry:]
    wbuf, tbuf, obuf, wsem, tsem, osem = refs[n + 1 :]
    z, x, c, y = (lax.axis_index(a) for a in ("z", "x", "c", "y"))
    half = att.shape[1] // 2
    rows = att.shape[0]
    flip = y == 1
    low, high = att[:, :half], att[:, half:]
    left = jnp.concatenate([jnp.where(flip, high, low), jnp.where(flip, low, high)], axis=1)
    slots = wbuf.shape[0]

    def cols(s, dx, dc, r):
        zz = lax.rem(z - s + nz, nz)
        return pl.ds(pl.multiple_of(((zz * nr + r) * 4 + (x ^ dx) * 2 + (c ^ dc)) * bs, bs), bs)

    def load(b):
        (s, dx, dc), halves = plan[b]
        slot = b % slots
        cps = []
        for h, (ref, lead, pos) in enumerate(halves):
            src = weights[ref] if lead is None else weights[ref].at[lead]
            if pos is not None:
                side = y if pos == 0 else 1 - y
                src = src.at[pl.ds(pl.multiple_of(side * half, half), half)]
            cps.append(pltpu.make_async_copy(src, wbuf.at[slot, pl.ds(h * half, half)], wsem.at[slot, h]))
        for r in range(nr):
            cps.append(
                pltpu.make_async_copy(tok.at[:, cols(s, dx, dc, r)], tbuf.at[slot, :, pl.ds(r * bs, bs)], tsem.at[slot, r])
            )
        return cps

    def store(b):
        (s, dx, dc), _ = plan[b]
        slot = b % slots
        return [
            pltpu.make_async_copy(obuf.at[slot, :, pl.ds(r * bs, bs)], out.at[:, cols(s, dx, dc, r)], osem.at[slot, r])
            for r in range(nr)
        ]

    for b in range(min(slots, len(plan))):
        for cp in load(b):
            cp.start()
    for b in range(len(plan)):
        slot = b % slots
        for cp in load(b):
            cp.wait()
        if b >= slots:
            for cp in store(b - slots):
                cp.wait()
        v = jnp.dot(left, wbuf[slot], preferred_element_type=F32)
        obuf[slot] = (tbuf[slot].astype(F32) + v).astype(BF16)
        for cp in store(b):
            cp.start()
        if b + slots < len(plan):
            for cp in load(b + slots):
                cp.start()
    for b in range(max(0, len(plan) - slots), len(plan)):
        for cp in store(b):
            cp.wait()


def output(att, tokens, weights, plan, nz, nr, bs, base=None):
    anywhere = pl.BlockSpec(memory_space=pl.ANY)
    slots = 6
    rows, width = tokens.shape
    return pl.pallas_call(
        functools.partial(out_kernel, plan=plan, nz=nz, nr=nr, bs=bs, carry=int(base is not None)),
        in_specs=[pl.BlockSpec(memory_space=pltpu.VMEM)]
        + [anywhere] * (1 + len(weights) + (base is not None)),
        input_output_aliases={} if base is None else {2 + len(weights): 0},
        out_specs=anywhere,
        out_shape=jax.ShapeDtypeStruct(tokens.shape, BF16),
        scratch_shapes=[
            pltpu.VMEM((slots, att.shape[1], nr * bs), BF16),
            pltpu.VMEM((slots, rows, nr * bs), BF16),
            pltpu.VMEM((slots, rows, nr * bs), BF16),
            pltpu.SemaphoreType.DMA((slots, 2)),
            pltpu.SemaphoreType.DMA((slots, nr)),
            pltpu.SemaphoreType.DMA((slots, nr)),
        ],
        compiler_params=params(12),
        cost_estimate=pl.CostEstimate(
            flops=2 * rows * nr * bs * len(plan) * att.shape[1],
            bytes_accessed=(att.shape[1] + 2 * rows) * 2 * nr * bs * len(plan),
            transcendentals=0,
        ),
        name="output",
    )(att, tokens, *weights, *(() if base is None else (base,)))


def trig(lens, rows, head, nr):
    length = jnp.sum(jnp.where(jnp.arange(lens.shape[0], dtype=jnp.int32) == prompt_index(nr), lens, 0))
    positions = length.astype(F32) + jnp.arange(rows, dtype=F32)
    steps = jnp.arange(head // 2, dtype=F32) * (2.0 / head)
    freqs = jnp.exp(-jnp.log(jnp.float32(500000.0)) * steps)
    angles = positions[:, None] * freqs[None, :]
    cos, sin = jnp.cos(angles), jnp.sin(angles)
    return jnp.stack([jnp.concatenate([cos, cos], axis=1), jnp.concatenate([-sin, sin], axis=1)])


def body(tokens, gain, w_query, w_key_value, w_out, cache_kv, cached_len, *, nz, nr):
    rows = tokens.shape[0]
    head = w_key_value.shape[1] // 2
    heads = w_query.shape[1] // head
    bs = w_query.shape[0]
    y = lax.axis_index("y")
    def swap(v, axis):
        return lax.ppermute(v, axis, [(0, 1), (1, 0)])

    def ring(v):
        return lax.ppermute(v, "z", [(i, (i + 1) % nz) for i in range(nz)])

    own_q, own_kv, own_o = w_query, w_key_value, w_out
    if nr > 1:
        own_q = lax.all_gather(own_q, "r", axis=0, tiled=True)
        own_kv = lax.all_gather(own_kv, "r", axis=0, tiled=True)
        own_o = lax.all_gather(own_o, "r", axis=1, tiled=True)
    half = own_q.shape[0] // 2
    ohalf = own_o.shape[0] // 2

    def tie(v, *after):
        return lax.optimization_barrier((v,) + after)[0]

    width = own_q.shape[1]
    with jax.named_scope("Ox"):
        x_o = swap(own_o, "x")
    (w_mine,) = gather(
        (own_q, own_kv),
        ((half, 2 * width),),
        ((0, 0, half, 2, None, (0, width)), (1, 0, half, 2, None, (width, width))),
        "pick",
        56,
        pltpu.VMEM,
    )
    toks = normalise(tokens, tie(gain, w_mine), nz, nr, bs)

    def step_z(v, name, *after):
        with jax.named_scope("Z" + name):
            return ring(tie(v, *after) if after else v)

    def step_y(v, name, *after):
        with jax.named_scope("Y" + name):
            return swap(tie(v, *after) if after else v, "y")

    w_near, w_far = [None], [None]
    with jax.named_scope("Tc"):
        core_toks = swap(toks[1], "c")
    with jax.named_scope("Tx"):
        across = swap(toks[2], "x")
    with jax.named_scope("Txc"):
        corner = lax.ppermute(toks[3], ("x", "c"), [(i, i ^ 3) for i in range(4)])
    with jax.named_scope("Oc0"):
        own_o_c = swap(own_o, "c")
        x_o_c = swap(x_o, "c")
    (pair,) = gather(
        (own_o, x_o),
        ((2, ohalf, own_o.shape[1]),),
        ((0, 0, ohalf, 2, 0, None), (1, 0, ohalf, 2, 1, None)),
        "pair",
        4,
        pltpu.VMEM,
    )
    v = w_mine
    turns = None
    for s in range(1, nz):
        if s == nz - 1:
            turns = trig(tie(cached_len, w_near[1]), rows, head, nr)
        after = [w_far[s - 2], core_toks, own_o_c, x_o_c, turns] if s == 3 else []
        v = step_z(v, f"w{s}", *after)
        w_near.append(v)
        w_far.append(step_y(v, f"w{s}", *(w_far[2:] if s == 3 else [])))

    def weights_of(steps):
        weights, halves = [], []
        for s in steps:
            if s == 0:
                weights.append((own_q, own_kv))
                halves.append((0, None, 2))
                continue
            for side, held in enumerate((w_near, w_far)):
                weights.append((held[s],))
                halves.append((s - steps[0], side, 1))
        return weights, halves

    o_near, o_far = [None], [None]
    o_near.append(step_z(pair, "o1", across))
    held = [toks[0], core_toks, across, tie(corner, o_near[1])]
    parts = project(held, *weights_of(range(nz)))
    o_near.append(step_z(o_near[1], "o2"))
    o_far.append(step_y(o_near[1], "o1"))
    with jax.named_scope("Pc"):
        from_c = swap(tie(parts[1], o_near[2], o_far[1]), "c")
    total = parts[2] + from_c[1]
    with jax.named_scope("Px"):
        other = swap(total, "x")
    o_near.append(step_z(o_near[2], "o3"))
    o_far.append(step_y(o_near[2], "o2"))
    last_far = [step_y(o_near[3][0], "o3"), step_z(o_far[2][1], "f3")]
    with jax.named_scope("Oc1"):
        near1_c = swap(tie(o_near[1], other), "c")
        far1_c = swap(tie(o_far[1], other), "c")

    att = attend(
        cached_len,
        parts[0],
        from_c,
        tie(other, o_near[3], o_far[2]),
        turns,
        cache_kv,
        heads,
        head,
        nr,
    )

    def over(v, dc, *after):
        if not dc:
            return v
        with jax.named_scope("Oc"):
            return swap(tie(v, *after), "c")

    def group(entries):
        weights, plan = [], []
        for place, halves in entries:
            spots = []
            for v, lead, pos in halves:
                at = [i for i, w in enumerate(weights) if w is v]
                if not at:
                    weights.append(v)
                    at = [len(weights) - 1]
                spots.append((at[0], lead, pos))
            plan.append((place, spots))
        return weights, plan

    def blocks(s, dc, near, far):
        return [((s, dx, dc), [(near, dx, None), (far, dx, None)]) for dx in range(2)]

    early, late = [], []
    for dc in range(2):
        for dx, v in enumerate(((own_o, x_o), (own_o_c, x_o_c))[dc]):
            early.append(((0, dx, dc), [(v, None, 0), (v, None, 1)]))
    early += blocks(1, 0, o_near[1], o_far[1]) + blocks(1, 1, near1_c, far1_c) + blocks(2, 0, o_near[2], o_far[2])
    out = output(att, tokens, *group(early), nz, nr, bs)
    late += blocks(2, 1, over(o_near[2], 1, att), over(o_far[2], 1, att))
    for dc in range(2):
        near = over(o_near[3], dc, att)
        for dx in range(2):
            late.append(((3, dx, dc), [(near, dx, None), (over(last_far[dx], dc, att), None, None)]))
    return output(att, tokens, *group(late), nz, nr, bs, out)


def solution(mesh):
    groups, blk = mesh.shape["groups"], mesh.shape["blk"]
    nz = 4
    nr = blk // (4 * nz)
    wide = Mesh(mesh.devices.reshape(groups, nz, nr, 2, 2), AXES)
    blocks = ("z", "r", "x", "c")
    placed = (
        P(AXES, None),
        P(),
        P(blocks, None),
        P(blocks, None),
        P(None, blocks),
        P(AXES, None, None),
        P("y"),
    )
    return jax.shard_map(
        functools.partial(body, nz=nz, nr=nr),
        mesh=wide,
        in_specs=placed,
        out_specs=P(AXES, None),
        check_vma=False,
    )
```

```python
import functools
import math

import jax
import jax.numpy as jnp
from jax import lax
from jax.experimental import pallas as pl
from jax.experimental.pallas import tpu as pltpu
from jax.sharding import Mesh, PartitionSpec as P

F32 = jnp.float32
BF16 = jnp.bfloat16
AXES = ("y", "z", "r", "x", "c")


def params(mib):
    return pltpu.CompilerParams(vmem_limit_bytes=mib * 1024 * 1024)


def gather_kernel(*refs, jobs):
    y = lax.axis_index("y")
    sem = refs[-1]
    copies = []
    for i, (src, side, rows, dst, lead, cols) in enumerate(jobs):
        ref, to = refs[src], refs[dst]
        if side is not None:
            ref = ref.at[pl.ds(pl.multiple_of((y if side == 0 else 1 - y) * rows, rows), rows)]
        if lead is not None:
            to = to.at[lead]
        if cols is not None:
            to = to.at[:, pl.ds(*cols)]
        copies.append(pltpu.make_async_copy(ref, to, sem.at[i]))
    for cp in copies:
        cp.start()
    for cp in copies:
        cp.wait()


def gather(arrays, shapes, jobs, name, limit, space):
    anywhere = pl.BlockSpec(memory_space=pl.ANY)
    size = sum(math.prod(shape) for shape in shapes)
    return pl.pallas_call(
        functools.partial(gather_kernel, jobs=jobs),
        in_specs=[anywhere] * len(arrays),
        out_specs=[pl.BlockSpec(memory_space=space)] * len(shapes),
        out_shape=[jax.ShapeDtypeStruct(shape, BF16) for shape in shapes],
        scratch_shapes=[pltpu.SemaphoreType.DMA((len(jobs),))],
        compiler_params=params(limit),
        cost_estimate=pl.CostEstimate(flops=0, bytes_accessed=4 * size, transcendentals=0),
        name=name,
    )(*arrays)


def norm_kernel(tokens, gain, *refs, nz, nr, bs, block):
    z, x, c = (lax.axis_index(a) for a in ("z", "x", "c"))
    outs, tbuf, sem = refs[:4], refs[4], refs[5]
    n = pl.program_id(0)

    def load(i):
        return pltpu.make_async_copy(tokens.at[pl.ds(i * block, block)], tbuf.at[i], sem.at[i])

    @pl.when(n == 0)
    def _():
        for i in range(tbuf.shape[0]):
            load(i).start()

    load(n).wait()
    tok = tbuf.at[n]
    width = tok.shape[1]
    step = 1024
    for r0 in range(0, block, 16):
        rows = pl.ds(r0, 16)
        acc = jnp.zeros((16, step), F32)
        for j in range(width // step):
            v = tok[rows, pl.ds(j * step, step)].astype(F32)
            acc = acc + v * v
        inv = lax.rsqrt(jnp.sum(acc, axis=1, keepdims=True) * (1.0 / width) + 1e-05)
        for k, out in enumerate(outs):
            part = (x ^ (k // 2)) * 2 + (c ^ (k % 2))
            for s in range(nz):
                zz = lax.rem(z - s + nz, nz)
                for r in range(nr):
                    cols = pl.ds(pl.multiple_of(((zz * nr + r) * 4 + part) * bs, bs), bs)
                    v = tok[rows, cols].astype(F32) * inv * gain[:, cols]
                    out[rows, pl.ds((s * nr + r) * bs, bs)] = v.astype(BF16)


def normalise(tokens, gain, nz, nr, bs):
    rows, width = tokens.shape
    block = 32
    quarter = width // 4
    return pl.pallas_call(
        functools.partial(norm_kernel, nz=nz, nr=nr, bs=bs, block=block),
        grid=(rows // block,),
        in_specs=[pl.BlockSpec(memory_space=pl.ANY), pl.BlockSpec((1, width), lambda i: (0, 0))],
        out_specs=[pl.BlockSpec((block, quarter), lambda i: (i, 0))] * 4,
        out_shape=[jax.ShapeDtypeStruct((rows, quarter), BF16)] * 4,
        scratch_shapes=[pltpu.VMEM((rows // block, block, width), BF16), pltpu.SemaphoreType.DMA((rows // block,))],
        compiler_params=params(56),
        cost_estimate=pl.CostEstimate(flops=8 * rows * width, bytes_accessed=rows * width, transcendentals=0),
        name="norm",
    )(tokens, gain.reshape(1, width))


def project_kernel(*refs, halves):
    toks, refs = refs[:4], refs[4:]
    count = sum(pieces for _, _, pieces in halves)
    weights, refs = list(refs[:count]), refs[count:]
    (mine, core, square), (tbuf, wbuf, tsem, wsem) = refs[:3], refs[3:]
    outs = (mine, core.at[0], square, core.at[1])
    y = lax.axis_index("y")
    rows = mine.shape[0]
    steps, both, width = wbuf.shape
    half = both // 2
    tcopies, wcopies = [], [[] for _ in range(steps)]
    for step in range(steps):
        cols = pl.ds(step * both, both)
        tcopies.append(
            [
                pltpu.make_async_copy(
                    toks[i].at[:, cols], tbuf.at[pl.ds(i * rows, rows), cols], tsem.at[step, i]
                )
                for i in range(4)
            ]
        )
    for n, (step, far, pieces) in enumerate(halves):
        if far is None:
            span = pl.ds(0, both)
        else:
            span = pl.ds(pl.multiple_of((1 - y if far else y) * half, half), half)
        for j in range(pieces):
            size = width // pieces
            to = wbuf.at[step, span, pl.ds(j * size, size)]
            wcopies[step].append(pltpu.make_async_copy(weights.pop(0), to, wsem.at[n, j]))
    for step in range(steps):
        for cp in tcopies[step] + wcopies[step]:
            cp.start()
    for step in range(steps):
        for cp in tcopies[step] + wcopies[step]:
            cp.wait()
        v = jnp.dot(tbuf[:, step * both : (step + 1) * both], wbuf[step], preferred_element_type=F32)
        for i in range(4):
            part = v[i * rows : (i + 1) * rows]
            if step:
                outs[i][...] += part
            else:
                outs[i][...] = part


def project(toks, weights, halves):
    rows, depth = toks[0].shape
    steps = 1 + max(step for step, _, _ in halves)
    both = depth // steps
    width = sum(w.shape[1] for w in weights[0])
    anywhere = pl.BlockSpec(memory_space=pl.ANY)
    vmem = pl.BlockSpec(memory_space=pltpu.VMEM)
    flat = [w for pair in weights for w in pair]
    shapes = [(rows, width), (2, rows, width), (rows, width)]
    return pl.pallas_call(
        functools.partial(project_kernel, halves=halves),
        in_specs=[anywhere] * (4 + len(flat)),
        out_specs=[vmem] * 3,
        out_shape=[jax.ShapeDtypeStruct(shape, F32) for shape in shapes],
        scratch_shapes=[
            pltpu.VMEM((4 * rows, depth), BF16),
            pltpu.VMEM((steps, both, width), BF16),
            pltpu.SemaphoreType.DMA((steps, 4)),
            pltpu.SemaphoreType.DMA((len(halves), 2)),
        ],
        compiler_params=params(16),
        cost_estimate=pl.CostEstimate(
            flops=2 * 4 * rows * depth * width, bytes_accessed=2 * 1024 * 1024, transcendentals=0
        ),
        name="project",
    )(*toks, *flat)


def prompt_index(nr):
    z, r, x, c = (lax.axis_index(a) for a in ("z", "r", "x", "c"))
    return ((z * nr + r) * 2 + x) * 2 + c


CHUNK = 1024


def cache_copies(cache, kvbuf, sem, base):
    return [
        pltpu.make_async_copy(
            cache.at[0, pl.ds(base + i * CHUNK, CHUNK)], kvbuf.at[pl.ds(i * CHUNK, CHUNK)], sem.at[i]
        )
        for i in range(kvbuf.shape[0] // CHUNK)
    ]


def scores(q, keys):
    return lax.dot_general(q, keys, (((1,), (1,)), ((), ())), preferred_element_type=F32)


def fold(q, copies, kvbuf, base, length, scale, top, total, acc):
    head = q.shape[1]
    for i, cp in enumerate(copies):
        cp.wait()
        s = scores(q, kvbuf[pl.ds(i * CHUNK, CHUNK), :head])
        col = lax.broadcasted_iota(jnp.int32, (1, CHUNK), 1) + (base + i * CHUNK)
        s = jnp.where(col < length, s, -1e30)
        new_top = jnp.maximum(top, jnp.max(s, axis=1, keepdims=True))
        p = jnp.exp2((s - new_top) * scale)
        fade = jnp.exp2((top - new_top) * scale)
        top = new_top
        total = total * fade + jnp.sum(p, axis=1, keepdims=True)
        acc = acc * fade + jnp.dot(
            p.astype(BF16), kvbuf[pl.ds(i * CHUNK, CHUNK), head:], preferred_element_type=F32
        )
    return top, total, acc


def attend_first_kernel(lens, mine, core, other, turns, cache, q_out, state, pbuf, kvbuf, psem, sem, *, heads, scale, nr):
    length = lens[prompt_index(nr)]
    rows = mine.shape[0]
    head = q_out.shape[1]
    copies = cache_copies(cache, kvbuf, sem, 0)
    sums = [
        pltpu.make_async_copy(ref, pbuf.at[i], psem.at[i]) for i, ref in enumerate((mine, core.at[0], other))
    ]
    for cp in sums + copies:
        cp.start()
    for cp in sums:
        cp.wait()
    total = (pbuf[0] + pbuf[1]) + pbuf[2]

    def turn(v):
        return (v * turns[0] + pltpu.roll(v, head // 2, 1) * turns[1]).astype(BF16)

    q = jnp.concatenate([turn(total[:, i * head : (i + 1) * head]) for i in range(heads)], axis=0)
    q_out[...] = q
    k_new = turn(total[:, heads * head : (heads + 1) * head])
    v_new = total[:, (heads + 1) * head :].astype(BF16)
    s = scores(q, k_new)
    row = lax.broadcasted_iota(jnp.int32, s.shape, 0) % rows
    col = lax.broadcasted_iota(jnp.int32, s.shape, 1)
    s = jnp.where(col <= row, s, -1e30)
    top = jnp.max(s, axis=1, keepdims=True)
    p = jnp.exp2((s - top) * scale)
    sum_p = jnp.sum(p, axis=1, keepdims=True)
    acc = jnp.dot(p.astype(BF16), v_new, preferred_element_type=F32)
    top, sum_p, acc = fold(q, copies, kvbuf, 0, length, scale, top, sum_p, acc)
    state[0] = jnp.broadcast_to(top, acc.shape)
    state[1] = jnp.broadcast_to(sum_p, acc.shape)
    state[2] = acc


def attend_last_kernel(lens, q, state, cache, out, kvbuf, sem, *, heads, scale, nr, base):
    length = lens[prompt_index(nr)]
    rows = out.shape[0]
    head = q.shape[1]
    copies = cache_copies(cache, kvbuf, sem, base)
    for cp in copies:
        cp.start()
    _, total, acc = fold(
        q[...], copies, kvbuf, base, length, scale, state[0][:, :1], state[1][:, :1], state[2]
    )
    acc = (acc / total).astype(BF16)
    for i in range(heads):
        out[:, i * head : (i + 1) * head] = acc[i * rows : (i + 1) * rows]


def attend_scale(head):
    return (head ** -0.5) * 1.4426950408889634


def attend_first(lens, mine, core, other, turns, cache, heads, head, nr, count):
    vmem, anywhere = (pl.BlockSpec(memory_space=m) for m in (pltpu.VMEM, pl.ANY))
    rows = mine.shape[0]
    return pl.pallas_call(
        functools.partial(attend_first_kernel, heads=heads, scale=attend_scale(head), nr=nr),
        in_specs=[pl.BlockSpec(memory_space=pltpu.SMEM)] + [anywhere] * 3 + [vmem, anywhere],
        out_specs=[vmem] * 2,
        out_shape=[
            jax.ShapeDtypeStruct((heads * rows, head), BF16),
            jax.ShapeDtypeStruct((3, heads * rows, head), F32),
        ],
        scratch_shapes=[
            pltpu.VMEM((3,) + mine.shape, F32),
            pltpu.VMEM((count, 2 * head), BF16),
            pltpu.SemaphoreType.DMA((3,)),
            pltpu.SemaphoreType.DMA((count // CHUNK,)),
        ],
        compiler_params=params(20),
        cost_estimate=pl.CostEstimate(
            flops=4 * rows * heads * head * count, bytes_accessed=14 * 1024 * 1024, transcendentals=rows * heads * count
        ),
        name="attend_first",
    )(lens, mine, core, other, turns, cache)


def attend_last(lens, q, state, cache, heads, nr, base):
    vmem, anywhere = (pl.BlockSpec(memory_space=m) for m in (pltpu.VMEM, pl.ANY))
    rows, head = q.shape[0] // heads, q.shape[1]
    count = cache.shape[1] - base
    return pl.pallas_call(
        functools.partial(attend_last_kernel, heads=heads, scale=attend_scale(head), nr=nr, base=base),
        in_specs=[pl.BlockSpec(memory_space=pltpu.SMEM), vmem, vmem, anywhere],
        out_specs=vmem,
        out_shape=jax.ShapeDtypeStruct((rows, heads * head), BF16),
        scratch_shapes=[pltpu.VMEM((count, 2 * head), BF16), pltpu.SemaphoreType.DMA((count // CHUNK,))],
        compiler_params=params(20),
        cost_estimate=pl.CostEstimate(
            flops=4 * rows * heads * head * count, bytes_accessed=14 * 1024 * 1024, transcendentals=rows * heads * count
        ),
        name="attend_last",
    )(lens, q, state, cache)


def out_kernel(att, tok, *refs, plan, nz, nr, bs, carry):
    n = len(refs) - 6 - 1 - carry
    weights, out = refs[:n], refs[n + carry]
    refs = refs[carry:]
    wbuf, tbuf, obuf, wsem, tsem, osem = refs[n + 1 :]
    z, x, c, y = (lax.axis_index(a) for a in ("z", "x", "c", "y"))
    half = att.shape[1] // 2
    rows = att.shape[0]
    flip = y == 1
    low, high = att[:, :half], att[:, half:]
    left = jnp.concatenate([jnp.where(flip, high, low), jnp.where(flip, low, high)], axis=1)
    slots = wbuf.shape[0]

    def cols(s, dx, dc, r):
        zz = lax.rem(z - s + nz, nz)
        return pl.ds(pl.multiple_of(((zz * nr + r) * 4 + (x ^ dx) * 2 + (c ^ dc)) * bs, bs), bs)

    def load(b):
        (s, dx, dc), halves = plan[b]
        slot = b % slots
        cps = []
        for h, (ref, lead, pos) in enumerate(halves):
            src = weights[ref] if lead is None else weights[ref].at[lead]
            if pos is not None:
                side = y if pos == 0 else 1 - y
                src = src.at[pl.ds(pl.multiple_of(side * half, half), half)]
            cps.append(pltpu.make_async_copy(src, wbuf.at[slot, pl.ds(h * half, half)], wsem.at[slot, h]))
        for r in range(nr):
            cps.append(
                pltpu.make_async_copy(tok.at[:, cols(s, dx, dc, r)], tbuf.at[slot, :, pl.ds(r * bs, bs)], tsem.at[slot, r])
            )
        return cps

    def store(b):
        (s, dx, dc), _ = plan[b]
        slot = b % slots
        return [
            pltpu.make_async_copy(obuf.at[slot, :, pl.ds(r * bs, bs)], out.at[:, cols(s, dx, dc, r)], osem.at[slot, r])
            for r in range(nr)
        ]

    for b in range(min(slots, len(plan))):
        for cp in load(b):
            cp.start()
    for b in range(len(plan)):
        slot = b % slots
        for cp in load(b):
            cp.wait()
        if b >= slots:
            for cp in store(b - slots):
                cp.wait()
        v = jnp.dot(left, wbuf[slot], preferred_element_type=F32)
        obuf[slot] = (tbuf[slot].astype(F32) + v).astype(BF16)
        for cp in store(b):
            cp.start()
        if b + slots < len(plan):
            for cp in load(b + slots):
                cp.start()
    for b in range(max(0, len(plan) - slots), len(plan)):
        for cp in store(b):
            cp.wait()


def output(att, tokens, weights, plan, nz, nr, bs, base=None):
    anywhere = pl.BlockSpec(memory_space=pl.ANY)
    slots = 6
    rows, width = tokens.shape
    return pl.pallas_call(
        functools.partial(out_kernel, plan=plan, nz=nz, nr=nr, bs=bs, carry=int(base is not None)),
        in_specs=[pl.BlockSpec(memory_space=pltpu.VMEM)]
        + [anywhere] * (1 + len(weights) + (base is not None)),
        input_output_aliases={} if base is None else {2 + len(weights): 0},
        out_specs=anywhere,
        out_shape=jax.ShapeDtypeStruct(tokens.shape, BF16),
        scratch_shapes=[
            pltpu.VMEM((slots, att.shape[1], nr * bs), BF16),
            pltpu.VMEM((slots, rows, nr * bs), BF16),
            pltpu.VMEM((slots, rows, nr * bs), BF16),
            pltpu.SemaphoreType.DMA((slots, 2)),
            pltpu.SemaphoreType.DMA((slots, nr)),
            pltpu.SemaphoreType.DMA((slots, nr)),
        ],
        compiler_params=params(12),
        cost_estimate=pl.CostEstimate(
            flops=2 * rows * nr * bs * len(plan) * att.shape[1],
            bytes_accessed=(att.shape[1] + 2 * rows) * 2 * nr * bs * len(plan),
            transcendentals=0,
        ),
        name="output",
    )(att, tokens, *weights, *(() if base is None else (base,)))


def trig(lens, rows, head, nr):
    length = jnp.sum(jnp.where(jnp.arange(lens.shape[0], dtype=jnp.int32) == prompt_index(nr), lens, 0))
    positions = length.astype(F32) + jnp.arange(rows, dtype=F32)
    steps = jnp.arange(head // 2, dtype=F32) * (2.0 / head)
    freqs = jnp.exp(-jnp.log(jnp.float32(500000.0)) * steps)
    angles = positions[:, None] * freqs[None, :]
    cos, sin = jnp.cos(angles), jnp.sin(angles)
    return jnp.stack([jnp.concatenate([cos, cos], axis=1), jnp.concatenate([-sin, sin], axis=1)])


def body(tokens, gain, w_query, w_key_value, w_out, cache_kv, cached_len, *, nz, nr):
    rows = tokens.shape[0]
    head = w_key_value.shape[1] // 2
    heads = w_query.shape[1] // head
    bs = w_query.shape[0]
    y = lax.axis_index("y")
    def swap(v, axis):
        return lax.ppermute(v, axis, [(0, 1), (1, 0)])

    def ring(v):
        return lax.ppermute(v, "z", [(i, (i + 1) % nz) for i in range(nz)])

    own_q, own_kv, own_o = w_query, w_key_value, w_out
    if nr > 1:
        own_q = lax.all_gather(own_q, "r", axis=0, tiled=True)
        own_kv = lax.all_gather(own_kv, "r", axis=0, tiled=True)
        own_o = lax.all_gather(own_o, "r", axis=1, tiled=True)
    half = own_q.shape[0] // 2
    ohalf = own_o.shape[0] // 2

    def tie(v, *after):
        return lax.optimization_barrier((v,) + after)[0]

    width = own_q.shape[1]
    with jax.named_scope("Ox"):
        x_o = swap(own_o, "x")
    (w_mine,) = gather(
        (own_q, own_kv),
        ((half, 2 * width),),
        ((0, 0, half, 2, None, (0, width)), (1, 0, half, 2, None, (width, width))),
        "pick",
        56,
        pltpu.VMEM,
    )
    toks = normalise(tokens, tie(gain, w_mine), nz, nr, bs)

    def step_z(v, name, *after):
        with jax.named_scope("Z" + name):
            return ring(tie(v, *after) if after else v)

    def step_y(v, name, *after):
        with jax.named_scope("Y" + name):
            return swap(tie(v, *after) if after else v, "y")

    w_near, w_far = [None], [None]
    with jax.named_scope("Tc"):
        core_toks = swap(toks[1], "c")
    with jax.named_scope("Tx"):
        across = swap(toks[2], "x")
    with jax.named_scope("Txc"):
        corner = lax.ppermute(toks[3], ("x", "c"), [(i, i ^ 3) for i in range(4)])
    with jax.named_scope("Oc0"):
        own_o_c = swap(own_o, "c")
        x_o_c = swap(x_o, "c")
    (pair,) = gather(
        (own_o, x_o),
        ((2, ohalf, own_o.shape[1]),),
        ((0, 0, ohalf, 2, 0, None), (1, 0, ohalf, 2, 1, None)),
        "pair",
        4,
        pltpu.VMEM,
    )
    v = w_mine
    turns = None
    for s in range(1, nz):
        if s == nz - 1:
            turns = trig(tie(cached_len, w_near[1]), rows, head, nr)
        after = [w_far[s - 2], core_toks, own_o_c, x_o_c, turns] if s == 3 else []
        v = step_z(v, f"w{s}", *after)
        w_near.append(v)
        w_far.append(step_y(v, f"w{s}", *(w_far[2:] if s == 3 else [])))

    def weights_of(steps):
        weights, halves = [], []
        for s in steps:
            if s == 0:
                weights.append((own_q, own_kv))
                halves.append((0, None, 2))
                continue
            for side, held in enumerate((w_near, w_far)):
                weights.append((held[s],))
                halves.append((s - steps[0], side, 1))
        return weights, halves

    o_near, o_far = [None], [None]
    o_near.append(step_z(pair, "o1", across))
    held = [toks[0], core_toks, across, tie(corner, o_near[1])]
    parts = project(held, *weights_of(range(nz)))
    o_near.append(step_z(o_near[1], "o2"))
    o_far.append(step_y(o_near[1], "o1"))
    with jax.named_scope("Pc"):
        from_c = swap(tie(parts[1], o_near[2], o_far[1]), "c")
    total = parts[2] + from_c[1]
    with jax.named_scope("Px"):
        other = swap(total, "x")
    o_near.append(step_z(o_near[2], "o3"))
    o_far.append(step_y(o_near[2], "o2"))
    with jax.named_scope("Oc1"):
        near1_c = swap(tie(o_near[1], total), "c")
        far1_c = swap(tie(o_far[1], other), "c")

    begun = cache_kv.shape[1] // (2 * CHUNK) * CHUNK
    q, state = attend_first(cached_len, parts[0], from_c, other, turns, cache_kv, heads, head, nr, begun)
    last_far = [
        step_y(tie(o_near[3], state)[0], "o3"),
        step_z(tie(o_far[2], state)[1], "f3"),
    ]
    att = attend_last(cached_len, q, tie(state, o_near[3], o_far[2]), cache_kv, heads, nr, begun)

    def over(v, dc, *after):
        if not dc:
            return v
        with jax.named_scope("Oc"):
            return swap(tie(v, *after), "c")

    def group(entries):
        weights, plan = [], []
        for place, halves in entries:
            spots = []
            for v, lead, pos in halves:
                at = [i for i, w in enumerate(weights) if w is v]
                if not at:
                    weights.append(v)
                    at = [len(weights) - 1]
                spots.append((at[0], lead, pos))
            plan.append((place, spots))
        return weights, plan

    def blocks(s, dc, near, far):
        return [((s, dx, dc), [(near, dx, None), (far, dx, None)]) for dx in range(2)]

    early, late = [], []
    for dc in range(2):
        for dx, v in enumerate(((own_o, x_o), (own_o_c, x_o_c))[dc]):
            early.append(((0, dx, dc), [(v, None, 0), (v, None, 1)]))
    early += blocks(1, 0, o_near[1], o_far[1]) + blocks(1, 1, near1_c, far1_c) + blocks(2, 0, o_near[2], o_far[2])
    out = output(att, tokens, *group(early), nz, nr, bs)
    late += blocks(2, 1, over(o_near[2], 1, att), over(o_far[2], 1, att))
    for dc in range(2):
        near = over(o_near[3], dc, att)
        for dx in range(2):
            late.append(((3, dx, dc), [(near, dx, None), (over(last_far[dx], dc, out), None, None)]))
    return output(att, tokens, *group(late), nz, nr, bs, out)


def solution(mesh):
    groups, blk = mesh.shape["groups"], mesh.shape["blk"]
    nz = 4
    nr = blk // (4 * nz)
    wide = Mesh(mesh.devices.reshape(groups, nz, nr, 2, 2), AXES)
    blocks = ("z", "r", "x", "c")
    placed = (
        P(AXES, None),
        P(),
        P(blocks, None),
        P(blocks, None),
        P(None, blocks),
        P(AXES, None, None),
        P("y"),
    )
    return jax.shard_map(
        functools.partial(body, nz=nz, nr=nr),
        mesh=wide,
        in_specs=placed,
        out_specs=P(AXES, None),
        check_vma=False,
    )
```

```python
import functools
import math

import jax
import jax.numpy as jnp
from jax import lax
from jax.experimental import pallas as pl
from jax.experimental.pallas import tpu as pltpu
from jax.sharding import Mesh, PartitionSpec as P

F32 = jnp.float32
BF16 = jnp.bfloat16
AXES = ("y", "z", "r", "x", "c")


def along(v):
    return v ^ (v >> 1)


def params(mib):
    return pltpu.CompilerParams(vmem_limit_bytes=mib * 1024 * 1024)


def gather_kernel(*refs, jobs):
    y = lax.axis_index("y")
    sem = refs[-1]
    copies = []
    for i, (src, side, rows, dst, lead, cols) in enumerate(jobs):
        ref, to = refs[src], refs[dst]
        if side is not None:
            ref = ref.at[pl.ds(pl.multiple_of((y if side == 0 else 1 - y) * rows, rows), rows)]
        if lead is not None:
            to = to.at[lead]
        if cols is not None:
            to = to.at[:, pl.ds(*cols)]
        copies.append(pltpu.make_async_copy(ref, to, sem.at[i]))
    for cp in copies:
        cp.start()
    for cp in copies:
        cp.wait()


def gather(arrays, shapes, jobs, name, limit, space):
    anywhere = pl.BlockSpec(memory_space=pl.ANY)
    size = sum(math.prod(shape) for shape in shapes)
    return pl.pallas_call(
        functools.partial(gather_kernel, jobs=jobs),
        in_specs=[anywhere] * len(arrays),
        out_specs=[pl.BlockSpec(memory_space=space)] * len(shapes),
        out_shape=[jax.ShapeDtypeStruct(shape, BF16) for shape in shapes],
        scratch_shapes=[pltpu.SemaphoreType.DMA((len(jobs),))],
        compiler_params=params(limit),
        cost_estimate=pl.CostEstimate(flops=0, bytes_accessed=4 * size, transcendentals=0),
        name=name,
    )(*arrays)


def norm_kernel(tokens, gain, *refs, nz, nr, bs, block):
    z, x, c = (lax.axis_index(a) for a in ("z", "x", "c"))
    outs, tbuf, sem = refs[:4], refs[4], refs[5]
    n = pl.program_id(0)

    def load(i):
        return pltpu.make_async_copy(tokens.at[pl.ds(i * block, block)], tbuf.at[i], sem.at[i])

    @pl.when(n == 0)
    def _():
        for i in range(tbuf.shape[0]):
            load(i).start()

    load(n).wait()
    tok = tbuf.at[n]
    width = tok.shape[1]
    step = 1024
    for r0 in range(0, block, 16):
        rows = pl.ds(r0, 16)
        acc = jnp.zeros((16, step), F32)
        for j in range(width // step):
            v = tok[rows, pl.ds(j * step, step)].astype(F32)
            acc = acc + v * v
        inv = lax.rsqrt(jnp.sum(acc, axis=1, keepdims=True) * (1.0 / width) + 1e-05)
        for k, out in enumerate(outs):
            part = (x ^ (k // 2)) * 2 + (c ^ (k % 2))
            for s in range(nz):
                zz = along(lax.rem(along(z) - s + nz, nz))
                for r in range(nr):
                    cols = pl.ds(pl.multiple_of(((zz * nr + r) * 4 + part) * bs, bs), bs)
                    v = tok[rows, cols].astype(F32) * inv * gain[:, cols]
                    out[rows, pl.ds((s * nr + r) * bs, bs)] = v.astype(BF16)


def normalise(tokens, gain, nz, nr, bs):
    rows, width = tokens.shape
    block = 32
    quarter = width // 4
    return pl.pallas_call(
        functools.partial(norm_kernel, nz=nz, nr=nr, bs=bs, block=block),
        grid=(rows // block,),
        in_specs=[pl.BlockSpec(memory_space=pl.ANY), pl.BlockSpec((1, width), lambda i: (0, 0))],
        out_specs=[pl.BlockSpec((block, quarter), lambda i: (i, 0))] * 4,
        out_shape=[jax.ShapeDtypeStruct((rows, quarter), BF16)] * 4,
        scratch_shapes=[pltpu.VMEM((rows // block, block, width), BF16), pltpu.SemaphoreType.DMA((rows // block,))],
        compiler_params=params(56),
        cost_estimate=pl.CostEstimate(flops=8 * rows * width, bytes_accessed=rows * width, transcendentals=0),
        name="norm",
    )(tokens, gain.reshape(1, width))


def project_kernel(*refs, halves):
    toks, refs = refs[:4], refs[4:]
    count = sum(pieces for _, _, pieces in halves)
    weights, refs = list(refs[:count]), refs[count:]
    (mine, core, square), (tbuf, wbuf, tsem, wsem) = refs[:3], refs[3:]
    outs = (mine, core.at[0], square, core.at[1])
    y = lax.axis_index("y")
    rows = mine.shape[0]
    steps, both, width = wbuf.shape
    half = both // 2
    tcopies, wcopies = [], [[] for _ in range(steps)]
    for step in range(steps):
        cols = pl.ds(step * both, both)
        tcopies.append(
            [
                pltpu.make_async_copy(
                    toks[i].at[:, cols], tbuf.at[pl.ds(i * rows, rows), cols], tsem.at[step, i]
                )
                for i in range(4)
            ]
        )
    for n, (step, far, pieces) in enumerate(halves):
        if far is None:
            span = pl.ds(0, both)
        else:
            span = pl.ds(pl.multiple_of((1 - y if far else y) * half, half), half)
        for j in range(pieces):
            size = width // pieces
            to = wbuf.at[step, span, pl.ds(j * size, size)]
            wcopies[step].append(pltpu.make_async_copy(weights.pop(0), to, wsem.at[n, j]))
    for step in range(steps):
        for cp in tcopies[step] + wcopies[step]:
            cp.start()
    for step in range(steps):
        for cp in tcopies[step] + wcopies[step]:
            cp.wait()
        v = jnp.dot(tbuf[:, step * both : (step + 1) * both], wbuf[step], preferred_element_type=F32)
        for i in range(4):
            part = v[i * rows : (i + 1) * rows]
            if step:
                outs[i][...] += part
            else:
                outs[i][...] = part


def project(toks, weights, halves):
    rows, depth = toks[0].shape
    steps = 1 + max(step for step, _, _ in halves)
    both = depth // steps
    width = sum(w.shape[1] for w in weights[0])
    anywhere = pl.BlockSpec(memory_space=pl.ANY)
    vmem = pl.BlockSpec(memory_space=pltpu.VMEM)
    flat = [w for pair in weights for w in pair]
    shapes = [(rows, width), (2, rows, width), (rows, width)]
    return pl.pallas_call(
        functools.partial(project_kernel, halves=halves),
        in_specs=[anywhere] * (4 + len(flat)),
        out_specs=[vmem] * 3,
        out_shape=[jax.ShapeDtypeStruct(shape, F32) for shape in shapes],
        scratch_shapes=[
            pltpu.VMEM((4 * rows, depth), BF16),
            pltpu.VMEM((steps, both, width), BF16),
            pltpu.SemaphoreType.DMA((steps, 4)),
            pltpu.SemaphoreType.DMA((len(halves), 2)),
        ],
        compiler_params=params(16),
        cost_estimate=pl.CostEstimate(
            flops=2 * 4 * rows * depth * width, bytes_accessed=2 * 1024 * 1024, transcendentals=0
        ),
        name="project",
    )(*toks, *flat)


def prompt_index(nr):
    z, r, x, c = (lax.axis_index(a) for a in ("z", "r", "x", "c"))
    return ((z * nr + r) * 2 + x) * 2 + c


CHUNK = 1024


def cache_copies(cache, kvbuf, sem, base):
    return [
        pltpu.make_async_copy(
            cache.at[0, pl.ds(base + i * CHUNK, CHUNK)], kvbuf.at[pl.ds(i * CHUNK, CHUNK)], sem.at[i]
        )
        for i in range(kvbuf.shape[0] // CHUNK)
    ]


def scores(q, keys):
    return lax.dot_general(q, keys, (((1,), (1,)), ((), ())), preferred_element_type=F32)


def fold(q, copies, kvbuf, base, length, scale, top, total, acc):
    head = q.shape[1]
    for i, cp in enumerate(copies):
        cp.wait()
        s = scores(q, kvbuf[pl.ds(i * CHUNK, CHUNK), :head])
        col = lax.broadcasted_iota(jnp.int32, (1, CHUNK), 1) + (base + i * CHUNK)
        s = jnp.where(col < length, s, -1e30)
        new_top = jnp.maximum(top, jnp.max(s, axis=1, keepdims=True))
        p = jnp.exp2((s - new_top) * scale)
        fade = jnp.exp2((top - new_top) * scale)
        top = new_top
        total = total * fade + jnp.sum(p, axis=1, keepdims=True)
        acc = acc * fade + jnp.dot(
            p.astype(BF16), kvbuf[pl.ds(i * CHUNK, CHUNK), head:], preferred_element_type=F32
        )
    return top, total, acc


def attend_first_kernel(lens, mine, core, other, turns, cache, q_out, state, pbuf, kvbuf, psem, sem, *, heads, scale, nr):
    length = lens[prompt_index(nr)]
    rows = mine.shape[0]
    head = q_out.shape[1]
    copies = cache_copies(cache, kvbuf, sem, 0)
    sums = [
        pltpu.make_async_copy(ref, pbuf.at[i], psem.at[i]) for i, ref in enumerate((mine, core.at[0], other))
    ]
    for cp in sums + copies:
        cp.start()
    for cp in sums:
        cp.wait()
    total = (pbuf[0] + pbuf[1]) + pbuf[2]

    def turn(v):
        return (v * turns[0] + pltpu.roll(v, head // 2, 1) * turns[1]).astype(BF16)

    q = jnp.concatenate([turn(total[:, i * head : (i + 1) * head]) for i in range(heads)], axis=0)
    q_out[...] = q
    k_new = turn(total[:, heads * head : (heads + 1) * head])
    v_new = total[:, (heads + 1) * head :].astype(BF16)
    s = scores(q, k_new)
    row = lax.broadcasted_iota(jnp.int32, s.shape, 0) % rows
    col = lax.broadcasted_iota(jnp.int32, s.shape, 1)
    s = jnp.where(col <= row, s, -1e30)
    top = jnp.max(s, axis=1, keepdims=True)
    p = jnp.exp2((s - top) * scale)
    sum_p = jnp.sum(p, axis=1, keepdims=True)
    acc = jnp.dot(p.astype(BF16), v_new, preferred_element_type=F32)
    top, sum_p, acc = fold(q, copies, kvbuf, 0, length, scale, top, sum_p, acc)
    state[0] = jnp.broadcast_to(top, acc.shape)
    state[1] = jnp.broadcast_to(sum_p, acc.shape)
    state[2] = acc


def attend_last_kernel(lens, q, state, cache, out, kvbuf, sem, *, heads, scale, nr, base):
    length = lens[prompt_index(nr)]
    rows = out.shape[0]
    head = q.shape[1]
    copies = cache_copies(cache, kvbuf, sem, base)
    for cp in copies:
        cp.start()
    _, total, acc = fold(
        q[...], copies, kvbuf, base, length, scale, state[0][:, :1], state[1][:, :1], state[2]
    )
    acc = (acc / total).astype(BF16)
    for i in range(heads):
        out[:, i * head : (i + 1) * head] = acc[i * rows : (i + 1) * rows]


def attend_scale(head):
    return (head ** -0.5) * 1.4426950408889634


def attend_first(lens, mine, core, other, turns, cache, heads, head, nr, count):
    vmem, anywhere = (pl.BlockSpec(memory_space=m) for m in (pltpu.VMEM, pl.ANY))
    rows = mine.shape[0]
    return pl.pallas_call(
        functools.partial(attend_first_kernel, heads=heads, scale=attend_scale(head), nr=nr),
        in_specs=[pl.BlockSpec(memory_space=pltpu.SMEM)] + [anywhere] * 3 + [vmem, anywhere],
        out_specs=[vmem] * 2,
        out_shape=[
            jax.ShapeDtypeStruct((heads * rows, head), BF16),
            jax.ShapeDtypeStruct((3, heads * rows, head), F32),
        ],
        scratch_shapes=[
            pltpu.VMEM((3,) + mine.shape, F32),
            pltpu.VMEM((count, 2 * head), BF16),
            pltpu.SemaphoreType.DMA((3,)),
            pltpu.SemaphoreType.DMA((count // CHUNK,)),
        ],
        compiler_params=params(20),
        cost_estimate=pl.CostEstimate(
            flops=4 * rows * heads * head * count, bytes_accessed=14 * 1024 * 1024, transcendentals=rows * heads * count
        ),
        name="attend_first",
    )(lens, mine, core, other, turns, cache)


def attend_last(lens, q, state, cache, heads, nr, base):
    vmem, anywhere = (pl.BlockSpec(memory_space=m) for m in (pltpu.VMEM, pl.ANY))
    rows, head = q.shape[0] // heads, q.shape[1]
    count = cache.shape[1] - base
    return pl.pallas_call(
        functools.partial(attend_last_kernel, heads=heads, scale=attend_scale(head), nr=nr, base=base),
        in_specs=[pl.BlockSpec(memory_space=pltpu.SMEM), vmem, vmem, anywhere],
        out_specs=vmem,
        out_shape=jax.ShapeDtypeStruct((rows, heads * head), BF16),
        scratch_shapes=[pltpu.VMEM((count, 2 * head), BF16), pltpu.SemaphoreType.DMA((count // CHUNK,))],
        compiler_params=params(20),
        cost_estimate=pl.CostEstimate(
            flops=4 * rows * heads * head * count, bytes_accessed=14 * 1024 * 1024, transcendentals=rows * heads * count
        ),
        name="attend_last",
    )(lens, q, state, cache)


def out_kernel(att, tok, *refs, plan, nz, nr, bs, carry):
    n = len(refs) - 6 - 1 - carry
    weights, out = refs[:n], refs[n + carry]
    refs = refs[carry:]
    wbuf, tbuf, obuf, wsem, tsem, osem = refs[n + 1 :]
    z, x, c, y = (lax.axis_index(a) for a in ("z", "x", "c", "y"))
    half = att.shape[1] // 2
    rows = att.shape[0]
    flip = y == 1
    low, high = att[:, :half], att[:, half:]
    left = jnp.concatenate([jnp.where(flip, high, low), jnp.where(flip, low, high)], axis=1)
    slots = wbuf.shape[0]

    def cols(s, dx, dc, r):
        zz = along(lax.rem(along(z) - s + nz, nz))
        return pl.ds(pl.multiple_of(((zz * nr + r) * 4 + (x ^ dx) * 2 + (c ^ dc)) * bs, bs), bs)

    def load(b):
        (s, dx, dc), halves = plan[b]
        slot = b % slots
        cps = []
        for h, (ref, lead, pos) in enumerate(halves):
            src = weights[ref] if lead is None else weights[ref].at[lead]
            if pos is not None:
                side = y if pos == 0 else 1 - y
                src = src.at[pl.ds(pl.multiple_of(side * half, half), half)]
            cps.append(pltpu.make_async_copy(src, wbuf.at[slot, pl.ds(h * half, half)], wsem.at[slot, h]))
        for r in range(nr):
            cps.append(
                pltpu.make_async_copy(tok.at[:, cols(s, dx, dc, r)], tbuf.at[slot, :, pl.ds(r * bs, bs)], tsem.at[slot, r])
            )
        return cps

    def store(b):
        (s, dx, dc), _ = plan[b]
        slot = b % slots
        return [
            pltpu.make_async_copy(obuf.at[slot, :, pl.ds(r * bs, bs)], out.at[:, cols(s, dx, dc, r)], osem.at[slot, r])
            for r in range(nr)
        ]

    for b in range(min(slots, len(plan))):
        for cp in load(b):
            cp.start()
    for b in range(len(plan)):
        slot = b % slots
        for cp in load(b):
            cp.wait()
        if b >= slots:
            for cp in store(b - slots):
                cp.wait()
        v = jnp.dot(left, wbuf[slot], preferred_element_type=F32)
        obuf[slot] = (tbuf[slot].astype(F32) + v).astype(BF16)
        for cp in store(b):
            cp.start()
        if b + slots < len(plan):
            for cp in load(b + slots):
                cp.start()
    for b in range(max(0, len(plan) - slots), len(plan)):
        for cp in store(b):
            cp.wait()


def output(att, tokens, weights, plan, nz, nr, bs, base=None):
    anywhere = pl.BlockSpec(memory_space=pl.ANY)
    slots = 6
    rows, width = tokens.shape
    return pl.pallas_call(
        functools.partial(out_kernel, plan=plan, nz=nz, nr=nr, bs=bs, carry=int(base is not None)),
        in_specs=[pl.BlockSpec(memory_space=pltpu.VMEM)]
        + [anywhere] * (1 + len(weights) + (base is not None)),
        input_output_aliases={} if base is None else {2 + len(weights): 0},
        out_specs=anywhere,
        out_shape=jax.ShapeDtypeStruct(tokens.shape, BF16),
        scratch_shapes=[
            pltpu.VMEM((slots, att.shape[1], nr * bs), BF16),
            pltpu.VMEM((slots, rows, nr * bs), BF16),
            pltpu.VMEM((slots, rows, nr * bs), BF16),
            pltpu.SemaphoreType.DMA((slots, 2)),
            pltpu.SemaphoreType.DMA((slots, nr)),
            pltpu.SemaphoreType.DMA((slots, nr)),
        ],
        compiler_params=params(12),
        cost_estimate=pl.CostEstimate(
            flops=2 * rows * nr * bs * len(plan) * att.shape[1],
            bytes_accessed=(att.shape[1] + 2 * rows) * 2 * nr * bs * len(plan),
            transcendentals=0,
        ),
        name="output",
    )(att, tokens, *weights, *(() if base is None else (base,)))


def trig(lens, rows, head, nr):
    length = jnp.sum(jnp.where(jnp.arange(lens.shape[0], dtype=jnp.int32) == prompt_index(nr), lens, 0))
    positions = length.astype(F32) + jnp.arange(rows, dtype=F32)
    steps = jnp.arange(head // 2, dtype=F32) * (2.0 / head)
    freqs = jnp.exp(-jnp.log(jnp.float32(500000.0)) * steps)
    angles = positions[:, None] * freqs[None, :]
    cos, sin = jnp.cos(angles), jnp.sin(angles)
    return jnp.stack([jnp.concatenate([cos, cos], axis=1), jnp.concatenate([-sin, sin], axis=1)])


def body(tokens, gain, w_query, w_key_value, w_out, cache_kv, cached_len, *, nz, nr):
    rows = tokens.shape[0]
    head = w_key_value.shape[1] // 2
    heads = w_query.shape[1] // head
    bs = w_query.shape[0]
    y = lax.axis_index("y")
    def swap(v, axis):
        return lax.ppermute(v, axis, [(0, 1), (1, 0)])

    def ring(v):
        return lax.ppermute(v, "z", [(along(i), along((i + 1) % nz)) for i in range(nz)])

    own_q, own_kv, own_o = w_query, w_key_value, w_out
    if nr > 1:
        own_q = lax.all_gather(own_q, "r", axis=0, tiled=True)
        own_kv = lax.all_gather(own_kv, "r", axis=0, tiled=True)
        own_o = lax.all_gather(own_o, "r", axis=1, tiled=True)
    half = own_q.shape[0] // 2
    ohalf = own_o.shape[0] // 2

    def tie(v, *after):
        return lax.optimization_barrier((v,) + after)[0]

    width = own_q.shape[1]
    with jax.named_scope("Ox"):
        x_o = swap(own_o, "x")
    (w_mine,) = gather(
        (own_q, own_kv),
        ((half, 2 * width),),
        ((0, 0, half, 2, None, (0, width)), (1, 0, half, 2, None, (width, width))),
        "pick",
        56,
        pltpu.VMEM,
    )
    toks = normalise(tokens, tie(gain, w_mine), nz, nr, bs)

    def step_z(v, name, *after):
        with jax.named_scope("Z" + name):
            return ring(tie(v, *after) if after else v)

    def step_y(v, name, *after):
        with jax.named_scope("Y" + name):
            return swap(tie(v, *after) if after else v, "y")

    w_near, w_far = [None], [None]
    with jax.named_scope("Tc"):
        core_toks = swap(toks[1], "c")
    with jax.named_scope("Tx"):
        across = swap(toks[2], "x")
    with jax.named_scope("Txc"):
        corner = lax.ppermute(toks[3], ("x", "c"), [(i, i ^ 3) for i in range(4)])
    with jax.named_scope("Oc0"):
        own_o_c = swap(own_o, "c")
        x_o_c = swap(x_o, "c")
    (pair,) = gather(
        (own_o, x_o),
        ((2, ohalf, own_o.shape[1]),),
        ((0, 0, ohalf, 2, 0, None), (1, 0, ohalf, 2, 1, None)),
        "pair",
        4,
        pltpu.VMEM,
    )
    v = w_mine
    turns = None
    for s in range(1, nz):
        if s == nz - 1:
            turns = trig(tie(cached_len, w_near[1]), rows, head, nr)
        after = [w_far[s - 2], core_toks, own_o_c, x_o_c, turns] if s == 3 else []
        v = step_z(v, f"w{s}", *after)
        w_near.append(v)
        w_far.append(step_y(v, f"w{s}", *(w_far[2:] if s == 3 else [])))

    def weights_of(steps):
        weights, halves = [], []
        for s in steps:
            if s == 0:
                weights.append((own_q, own_kv))
                halves.append((0, None, 2))
                continue
            for side, held in enumerate((w_near, w_far)):
                weights.append((held[s],))
                halves.append((s - steps[0], side, 1))
        return weights, halves

    o_near, o_far = [None], [None]
    o_near.append(step_z(pair, "o1", across))
    held = [toks[0], core_toks, across, tie(corner, o_near[1])]
    parts = project(held, *weights_of(range(nz)))
    o_near.append(step_z(o_near[1], "o2"))
    o_far.append(step_y(o_near[1], "o1"))
    with jax.named_scope("Pc"):
        from_c = swap(tie(parts[1], o_near[2], o_far[1]), "c")
    total = parts[2] + from_c[1]
    with jax.named_scope("Px"):
        other = swap(total, "x")
    o_near.append(step_z(o_near[2], "o3"))
    o_far.append(step_y(o_near[2], "o2"))
    with jax.named_scope("Oc1"):
        near1_c = swap(tie(o_near[1], total), "c")
        far1_c = swap(tie(o_far[1], other), "c")

    begun = cache_kv.shape[1] // (2 * CHUNK) * CHUNK
    q, state = attend_first(cached_len, parts[0], from_c, other, turns, cache_kv, heads, head, nr, begun)
    last_far = [
        step_y(tie(o_near[3], state)[0], "o3"),
        step_z(tie(o_far[2], state)[1], "f3"),
    ]
    att = attend_last(cached_len, q, tie(state, o_near[3], o_far[2]), cache_kv, heads, nr, begun)

    def over(v, dc, *after):
        if not dc:
            return v
        with jax.named_scope("Oc"):
            return swap(tie(v, *after), "c")

    def group(entries):
        weights, plan = [], []
        for place, halves in entries:
            spots = []
            for v, lead, pos in halves:
                at = [i for i, w in enumerate(weights) if w is v]
                if not at:
                    weights.append(v)
                    at = [len(weights) - 1]
                spots.append((at[0], lead, pos))
            plan.append((place, spots))
        return weights, plan

    def blocks(s, dc, near, far):
        return [((s, dx, dc), [(near, dx, None), (far, dx, None)]) for dx in range(2)]

    early, late = [], []
    for dc in range(2):
        for dx, v in enumerate(((own_o, x_o), (own_o_c, x_o_c))[dc]):
            early.append(((0, dx, dc), [(v, None, 0), (v, None, 1)]))
    early += blocks(1, 0, o_near[1], o_far[1]) + blocks(1, 1, near1_c, far1_c) + blocks(2, 0, o_near[2], o_far[2])
    out = output(att, tokens, *group(early), nz, nr, bs)
    late += blocks(2, 1, over(o_near[2], 1, att), over(o_far[2], 1, att))
    for dc in range(2):
        near = over(o_near[3], dc, att)
        for dx in range(2):
            late.append(((3, dx, dc), [(near, dx, None), (over(last_far[dx], dc, out), None, None)]))
    return output(att, tokens, *group(late), nz, nr, bs, out)


def solution(mesh):
    groups, blk = mesh.shape["groups"], mesh.shape["blk"]
    nz = 4
    nr = blk // (4 * nz)
    wide = Mesh(mesh.devices.reshape(groups, nz, nr, 2, 2), AXES)
    blocks = ("z", "r", "x", "c")
    placed = (
        P(AXES, None),
        P(),
        P(blocks, None),
        P(blocks, None),
        P(None, blocks),
        P(AXES, None, None),
        P("y"),
    )
    return jax.shard_map(
        functools.partial(body, nz=nz, nr=nr),
        mesh=wide,
        in_specs=placed,
        out_specs=P(AXES, None),
        check_vma=False,
    )
```
